256 devices in a mesh: dp: 2 (over x_lo), resp: 16 (over z, core), tensor: 8 (over y, x_hi).
Axes of the slice: x: 4 (x_hi: 2, x_lo: 2; x = x_hi * 2 + x_lo), y: 4, z: 8, core: 2. Of those that a mesh axis runs over, the one named last changes fastest.
Arguments:
- queries: bfloat16 [8192, 8192], P(('dp', 'resp'), 'tensor'), parts along dimension 0, may hold values from -200 to 200
- resp_keys: bfloat16 [8192, 1024], P(('dp', 'resp'), 'tensor'), parts along dimension 0, may hold values from -6 to 6
- resp_values: bfloat16 [8192, 1024], P(('dp', 'resp'), 'tensor'), parts along dimension 0, may hold values from -6 to 6
- prompt_keys: bfloat16 [4096, 1024], P(('dp', 'resp'), 'tensor'), parts along dimension 0, may hold values from -6 to 6
- prompt_values: bfloat16 [4096, 1024], P(('dp', 'resp'), 'tensor'), parts along dimension 0, may hold values from -6 to 6
- out_grad: bfloat16 [8192, 8192], P(('dp', 'resp'), 'tensor'), parts along dimension 0, may hold values from -6 to 6
- pref_table: bfloat16 [16, 8192], P(None, 'tensor'), may hold values from -6 to 6
- pref_ids: int32 [32], P(('dp', 'resp')), parts along dimension 0, may hold values from 0 to 15
- resp_len: int32 [32], P(('dp', 'resp')), parts along dimension 0, may hold values from 1 to 256, 3072 in all
Outputs:
- query_grad: bfloat16 [8192, 8192], P(('dp', 'resp'), 'tensor'), parts along dimension 0
- resp_key_grad: bfloat16 [8192, 1024], P(('dp', 'resp'), 'tensor'), parts along dimension 0
- resp_value_grad: bfloat16 [8192, 1024], P(('dp', 'resp'), 'tensor'), parts along dimension 0
- prompt_key_grad: bfloat16 [4096, 1024], P(('dp', 'resp'), 'tensor'), parts along dimension 0
- prompt_value_grad: bfloat16 [4096, 1024], P(('dp', 'resp'), 'tensor'), parts along dimension 0
- pref_grad: float32 [32, 8192], P('dp', 'tensor'), parts along dimension 0
The draws below stay inside these ranges and needn't reach their ends.
There are 2 independent parts, one for each index of `dp`. The reference program is written for one: setup_inputs(seed, part) draws one part's arguments, and reference() takes and returns one part's arrays. A program takes and returns all parts, laid end to end along the dimension named above; an argument that names none is the same for every part. Nothing has to cross between parts.
Inputs may be any that keep to these rules, and one draw needn't show every extreme that they name: `resp_len`: in each group the lengths sum to 3072 and one of them is 256.
All inputs are finite; a program needn't handle non-finite values.
Results may differ from the reference program's by a relative error of at most 0.023.
Values may be sent and summed in bfloat16 or wider, within the bound.
No kernel may reach another device: no remote copies, remote signals or barrier semaphores. Data moves between devices by JAX's collectives and lax.ppermute only.
A program may use at most 64 MiB of HBM per device.

```python
import math
import jax
import jax.numpy as jnp
import numpy as np
from jax import lax

HEAD_DIM = 128
KV_HEADS = 8
GROUP = 8
HEADS = 64
RESP_LEN = 256
NPREF = 16
RESPONSES = 16
PROMPT = 2048
RESP_ROWS = 4096


def shared_keys(key):
    return jax.random.normal(key, (PROMPT, KV_HEADS * HEAD_DIM), jnp.float32)


def draw_prompt_keys(key, part):
    anchors = shared_keys(key)
    return jnp.clip(anchors, -6.0, 6.0).astype(jnp.bfloat16)


def draw_queries(key, part):
    key = jax.random.fold_in(key, 7)
    fresh = jnp.clip(jax.random.normal(key, (RESP_ROWS, HEADS * HEAD_DIM), jnp.float32), -6.0, 6.0)
    return fresh.astype(jnp.bfloat16)


def plant(values, key, low, high):
    longest = values.shape.index(max(values.shape))
    spots = []
    for shift in (0, 1):
        where = [jax.random.randint(jax.random.fold_in(key, axis), (), 0, length) for axis, length in enumerate(values.shape)]
        where[longest] = (where[longest] + shift) % values.shape[longest]
        spots.append(tuple(where))
    return values.at[spots[0]].set(low).at[spots[1]].set(high)


def block_levels(stream_key, shape, pieces, least, high):
    factor_of, own = 1.0, jax.random.fold_in(stream_key, 6)
    for dim, blocks in pieces:
        steps = jnp.exp(jax.random.uniform(jax.random.fold_in(own, dim), (blocks,), jnp.float32, least / len(pieces), high / len(pieces)))
        factor_of = factor_of * jnp.repeat(steps, shape[dim] // blocks).reshape([-1 if axis == dim else 1 for axis in range(len(shape))])
    return factor_of


def profile(count, total, bound, lean):
    portions = [(1 << 20) // math.isqrt(standing ** lean) + 1 for standing in range(2, count + 1)]
    spare, holding = total - bound - (count - 1), [1] * (count - 1)
    while spare > 0:
        free = [i for i in range(count - 1) if holding[i] < bound]
        mass, left = sum([portions[i] for i in free]), spare
        for i in free:
            more = min(bound - holding[i], max(1, left * portions[i] // mass), spare)
            holding[i] = holding[i] + more
            spare = spare - more
    return np.array([bound] + holding)


def uneven(own_key, number_of, total, reach, slope):
    if number_of == 2:
        one = jax.random.randint(own_key, (), max(1, total - reach), min(reach, total - 1) + 1)
        return jnp.stack([one, total - one])
    lengths = jnp.asarray(profile(number_of, total, reach, slope), jnp.int32)
    pairs = (number_of - 1) // 2
    giver, receiver = lengths[1:1 + 2 * pairs:2], lengths[2:2 + 2 * pairs:2]
    room = jnp.minimum(giver - 1, reach - receiver)
    moved = jax.random.randint(jax.random.fold_in(own_key, 1), (pairs,), 0, 1 << 20) % (room + 1)
    lengths = lengths.at[1:1 + 2 * pairs:2].set(giver - moved).at[2:2 + 2 * pairs:2].set(receiver + moved)
    return lengths[jax.random.permutation(jax.random.fold_in(own_key, 2), number_of)]


def centred(own_key, dims, scale, limit, pieces=(), kind=jnp.bfloat16):
    array = scale * jax.random.normal(own_key, dims, jnp.float32)
    if pieces:
        array = array * block_levels(own_key, dims, pieces, -0.22, 0.18)
    return jnp.clip(array, -limit, limit).astype(kind)


def setup_inputs(seed: int = 0, part: int = 0) -> dict:
    arg_keys = jax.random.split(jax.random.key(seed), 10)
    part_keys = jax.random.split(jax.random.fold_in(arg_keys[9], part), 10)
    queries = draw_queries(jax.random.fold_in(jax.random.fold_in(arg_keys[9], part), 71), part)
    resp_keys = centred(part_keys[1], (RESP_ROWS, KV_HEADS * HEAD_DIM), 1.0, 6.0, ((0, 16), (1, 8)))
    resp_values = centred(part_keys[2], (RESP_ROWS, KV_HEADS * HEAD_DIM), 1.0, 6.0, ((0, 16), (1, 8)))
    prompt_keys = draw_prompt_keys(jax.random.fold_in(jax.random.fold_in(arg_keys[9], part), 71), part)
    prompt_values = centred(part_keys[4], (PROMPT, KV_HEADS * HEAD_DIM), 1.0, 6.0, ((0, 16), (1, 8)))
    out_grad = centred(part_keys[5], (RESP_ROWS, HEADS * HEAD_DIM), 1.0, 6.0, ((0, 16), (1, 8)))
    pref_table = centred(arg_keys[6], (NPREF, HEADS * HEAD_DIM), 1.0, 6.0, ((1, 8),))
    pref_ids = plant(jax.random.randint(part_keys[7], (RESPONSES,), 0, NPREF), jax.random.fold_in(part_keys[7], 1), 0, NPREF - 1).astype(jnp.int32)
    resp_len = uneven(part_keys[8], RESPONSES, RESPONSES * RESP_LEN * 3 // 4, RESP_LEN, 2).astype(jnp.int32)
    return dict(queries=queries, resp_keys=resp_keys, resp_values=resp_values, prompt_keys=prompt_keys, prompt_values=prompt_values, out_grad=out_grad, pref_table=pref_table, pref_ids=pref_ids, resp_len=resp_len)


def head_grads(query_rows, grad_rows, key_block, value_block, visible, scaling):
    scores = jnp.dot(query_rows, key_block.T, preferred_element_type=jnp.float32) * scaling
    scores = jnp.where(visible, scores, -1e30)
    row_max = jnp.max(scores, axis=1, keepdims=True)
    exponent = jnp.exp(scores - row_max)
    weights = exponent / jnp.sum(exponent, axis=1, keepdims=True)
    low_weights = weights.astype(jnp.bfloat16)
    output = jnp.dot(low_weights, value_block, preferred_element_type=jnp.float32)
    row_delta = jnp.sum(grad_rows.astype(jnp.float32) * output, axis=1, keepdims=True)
    grad_weights = jnp.dot(grad_rows, value_block.T, preferred_element_type=jnp.float32)
    grad_scores = (weights * (grad_weights - row_delta)).astype(jnp.bfloat16)
    grad_query = jnp.dot(grad_scores, key_block, preferred_element_type=jnp.float32) * scaling
    grad_keys = jnp.dot(grad_scores.T, query_rows, preferred_element_type=jnp.float32) * scaling
    grad_values = jnp.dot(low_weights.T, grad_rows, preferred_element_type=jnp.float32)
    return grad_query, grad_keys, grad_values


def reference(queries, resp_keys, resp_values, prompt_keys, prompt_values, out_grad, pref_table, pref_ids, resp_len):
    scaling = HEAD_DIM ** -0.5
    key_span = PROMPT + RESP_LEN
    positions = jnp.arange(RESP_LEN, dtype=jnp.int32)
    causal = positions[:, None] >= positions[None, :]
    visible = jnp.concatenate([jnp.ones((RESP_LEN, PROMPT), bool), causal], axis=1)
    prompt_k = prompt_keys.reshape(PROMPT, KV_HEADS, HEAD_DIM)
    prompt_v = prompt_values.reshape(PROMPT, KV_HEADS, HEAD_DIM)

    def one_response(response):
        first_row = (response * RESP_LEN).astype(jnp.int32)
        own_queries = lax.dynamic_slice_in_dim(queries, first_row, RESP_LEN, 0)
        pref_vector = lax.dynamic_index_in_dim(pref_table, pref_ids[response], 0, keepdims=False)
        biased = (own_queries.astype(jnp.float32) + pref_vector.astype(jnp.float32)[None, :]).astype(jnp.bfloat16)
        biased = biased.reshape(RESP_LEN, HEADS, HEAD_DIM)
        is_valid = positions < resp_len[response]
        own_grad = lax.dynamic_slice_in_dim(out_grad, first_row, RESP_LEN, 0)
        masked_grad = jnp.where(is_valid[:, None], own_grad, jnp.zeros((), jnp.bfloat16)).reshape(RESP_LEN, HEADS, HEAD_DIM)
        own_keys = lax.dynamic_slice_in_dim(resp_keys, first_row, RESP_LEN, 0).reshape(RESP_LEN, KV_HEADS, HEAD_DIM)
        own_values = lax.dynamic_slice_in_dim(resp_values, first_row, RESP_LEN, 0).reshape(RESP_LEN, KV_HEADS, HEAD_DIM)
        all_keys = jnp.concatenate([prompt_k, own_keys], axis=0)
        all_values = jnp.concatenate([prompt_v, own_values], axis=0)

        def one_head(head_index):
            kv_head = (head_index // GROUP).astype(jnp.int32)
            query_rows = lax.dynamic_index_in_dim(biased, head_index, 1, keepdims=False)
            grad_rows = lax.dynamic_index_in_dim(masked_grad, head_index, 1, keepdims=False)
            key_block = lax.dynamic_index_in_dim(all_keys, kv_head, 1, keepdims=False)
            value_block = lax.dynamic_index_in_dim(all_values, kv_head, 1, keepdims=False)
            return head_grads(query_rows, grad_rows, key_block, value_block, visible, scaling)

        grad_query, grad_keys, grad_values = lax.map(one_head, jnp.arange(HEADS, dtype=jnp.int32))
        grad_keys = grad_keys.reshape(KV_HEADS, GROUP, key_span, HEAD_DIM).sum(axis=1)
        grad_values = grad_values.reshape(KV_HEADS, GROUP, key_span, HEAD_DIM).sum(axis=1)
        return grad_query, grad_keys, grad_values

    grad_query, grad_keys, grad_values = lax.map(one_response, jnp.arange(RESPONSES, dtype=jnp.int32))
    query_grad = grad_query.transpose(0, 2, 1, 3).reshape(RESP_ROWS, HEADS * HEAD_DIM).astype(jnp.bfloat16)
    row_sums = grad_query.sum(axis=2).reshape(RESPONSES, HEADS * HEAD_DIM)
    chosen = (pref_ids[:, None] == jnp.arange(NPREF, dtype=jnp.int32)[None, :]).astype(jnp.float32)
    pref_grad = jnp.dot(chosen.T, row_sums, precision=lax.Precision.HIGHEST)
    resp_key_grad = grad_keys[:, :, PROMPT:, :].transpose(0, 2, 1, 3).reshape(RESP_ROWS, KV_HEADS * HEAD_DIM).astype(jnp.bfloat16)
    resp_value_grad = grad_values[:, :, PROMPT:, :].transpose(0, 2, 1, 3).reshape(RESP_ROWS, KV_HEADS * HEAD_DIM).astype(jnp.bfloat16)
    prompt_key_grad = grad_keys[:, :, :PROMPT, :].sum(axis=0).transpose(1, 0, 2).reshape(PROMPT, KV_HEADS * HEAD_DIM).astype(jnp.bfloat16)
    prompt_value_grad = grad_values[:, :, :PROMPT, :].sum(axis=0).transpose(1, 0, 2).reshape(PROMPT, KV_HEADS * HEAD_DIM).astype(jnp.bfloat16)
    return (query_grad, resp_key_grad, resp_value_grad, prompt_key_grad, prompt_value_grad, pref_grad)
```

```python
import functools

import jax
import jax.numpy as jnp
from jax import lax
from jax.experimental import pallas as pl
from jax.experimental.pallas import tpu as pltpu
from jax.sharding import PartitionSpec as P

F32 = jnp.float32
BF16 = jnp.bfloat16
HEAD_DIM = 128
SCALING = HEAD_DIM**-0.5
LOG2E = 1.4426950408889634
HEADS_PER_STEP = 2
CHUNK = 256
RTILE = 16
NT = (((1,), (1,)), ((), ()))
NN = (((1,), (0,)), ((), ()))
VMEM = pl.BlockSpec(memory_space=pltpu.VMEM)
SMEM = pl.BlockSpec(memory_space=pltpu.SMEM)


def ring_moves(n_resp):
    chips = n_resp // 2

    def index(chip, core):
        return (chip % chips) * 2 + core

    places = [(chip, core) for chip in range(chips) for core in range(2)]
    pair = [(index(z, c), index(z, 1 - c)) for z, c in places]
    far = [(index(z, c), index(z + chips // 2, c)) for z, c in places]
    out = [
        [(index(z, c), index(z + k if c == 0 else z - k, c)) for z, c in places]
        for k in range(1, chips // 2)
    ]
    back = [[(b, a) for a, b in moves] for moves in out]
    return pair, far, out, back


def attention_kernel(
    n_blocks,
    id_ref,
    len_ref,
    q_ref,
    g_ref,
    table_ref,
    rk_ref,
    rv_ref,
    *refs,
):
    block_refs = refs[:n_blocks]
    dq_ref, drk_ref, drv_ref, near_ref, direct_ref, via_ref, r_ref = refs[n_blocks : n_blocks + 7]
    keys, values, keys_t, s_scr, p_scr, dk_scr, dv_scr, pref_scr, sum_scr = refs[n_blocks + 7 :]
    rows = q_ref.shape[0]
    heads = q_ref.shape[1] // HEAD_DIM
    n_keys = keys.shape[0]
    n_prompt = n_keys - rows
    width = HEADS_PER_STEP * rows
    at = 0
    for block in block_refs:
        n = block.shape[0]
        keys[at : at + n, :] = block[:, :HEAD_DIM]
        values[at : at + n, :] = block[:, HEAD_DIM:]
        at += n
    keys[n_prompt:, :] = rk_ref[...]
    values[n_prompt:, :] = rv_ref[...]
    keys_t[...] = keys[...].T
    dk_scr[...] = jnp.zeros_like(dk_scr)
    dv_scr[...] = jnp.zeros_like(dv_scr)
    chosen = lax.broadcasted_iota(jnp.int32, table_ref.shape, 0) == id_ref[0]
    pref_scr[...] = jnp.sum(
        jnp.where(chosen, table_ref[...].astype(F32), 0.0), axis=0, keepdims=True
    )
    live = lax.broadcasted_iota(jnp.int32, (rows, HEAD_DIM), 0) < len_ref[0]
    chunks = [(a, min(CHUNK, n_keys - a)) for a in range(0, n_keys, CHUNK)]
    factor = SCALING * LOG2E

    def step(group, carry):
        q_parts, g_parts = [], []
        for i in range(HEADS_PER_STEP):
            cols = pl.ds(
                pl.multiple_of((group * HEADS_PER_STEP + i) * HEAD_DIM, HEAD_DIM), HEAD_DIM
            )
            q_parts.append((q_ref[:, cols].astype(F32) + pref_scr[:, cols]).astype(BF16))
            g_parts.append(jnp.where(live, g_ref[:, cols], jnp.zeros((), BF16)))
        q = jnp.concatenate(q_parts, axis=0)
        g = jnp.concatenate(g_parts, axis=0)
        top = jnp.full((8, width), -1e30, F32)
        for a, n in chunks:
            s = lax.dot_general(keys[a : a + n, :], q, NT, preferred_element_type=F32)
            if a + n > n_prompt:
                key_pos = lax.broadcasted_iota(jnp.int32, (n, width), 0) + (a - n_prompt)
                query_pos = lax.broadcasted_iota(jnp.int32, (n, width), 1) % rows
                s = jnp.where(key_pos <= query_pos, s, -1e30)
            s_scr[a : a + n, :] = s
            top = jnp.maximum(top, jnp.max(s.reshape(n // 8, 8, width), axis=0))
        row_max = jnp.max(top, axis=0, keepdims=True) * factor
        total = jnp.zeros((8, width), F32)
        dot = jnp.zeros((8, width), F32)
        for a, n in chunks:
            p = jnp.exp2(s_scr[a : a + n, :] * factor - row_max)
            dp = lax.dot_general(values[a : a + n, :], g, NT, preferred_element_type=F32)
            total = total + jnp.sum(p.reshape(n // 8, 8, width), axis=0)
            dot = dot + jnp.sum((p * dp).reshape(n // 8, 8, width), axis=0)
            s_scr[a : a + n, :] = dp
            p_scr[a : a + n, :] = p
        inverse = 1.0 / jnp.sum(total, axis=0, keepdims=True)
        delta = jnp.sum(dot, axis=0, keepdims=True) * inverse
        dq = jnp.zeros((HEAD_DIM, width), F32)
        for a, n in chunks:
            w = p_scr[a : a + n, :] * inverse
            ds = (w * (s_scr[a : a + n, :] - delta)).astype(BF16)
            dv_scr[a : a + n, :] += lax.dot_general(
                w.astype(BF16), g, NN, preferred_element_type=F32
            )
            dk_scr[a : a + n, :] += lax.dot_general(ds, q, NN, preferred_element_type=F32)
            dq = dq + lax.dot_general(keys_t[:, a : a + n], ds, NN, preferred_element_type=F32)
        dq = dq.T * SCALING
        for i in range(HEADS_PER_STEP):
            cols = pl.ds(
                pl.multiple_of((group * HEADS_PER_STEP + i) * HEAD_DIM, HEAD_DIM), HEAD_DIM
            )
            part = dq[i * rows : (i + 1) * rows]
            dq_ref[:, cols] = part.astype(BF16)
            sum_scr[:, cols] = jnp.sum(part, axis=0, keepdims=True)
        return carry

    lax.fori_loop(0, heads // HEADS_PER_STEP, step, 0)

    at = 0
    for ref in (near_ref, direct_ref, via_ref):
        n = ref.shape[0]
        if ref is via_ref:
            n -= RTILE
        ref[:n, :HEAD_DIM] = (dk_scr[at : at + n, :] * SCALING).astype(BF16)
        ref[:n, HEAD_DIM:] = dv_scr[at : at + n, :].astype(BF16)
        at += n
    drk_ref[...] = (dk_scr[n_prompt:, :] * SCALING).astype(BF16)
    drv_ref[...] = dv_scr[n_prompt:, :].astype(BF16)
    lanes = 2 * HEAD_DIM
    pieces = [sum_scr[:, j * lanes : (j + 1) * lanes] for j in range(heads // 2)]
    hot = (lax.broadcasted_iota(jnp.int32, (1, lanes), 1) == id_ref[0]).astype(F32)
    tile = jnp.concatenate(
        pieces + [hot, jnp.zeros((RTILE - heads // 2 - 1, lanes), F32)], axis=0
    ).astype(BF16)
    r_ref[...] = tile
    via_ref[via_ref.shape[0] - RTILE :, :] = tile


def attention(pref_ids, resp_len, queries, out_grad, table, resp_keys, resp_values, blocks):
    rows = queries.shape[0]
    block = blocks[0].shape[0] // 2
    n_prompt = sum(b.shape[0] for b in blocks)
    n_keys = n_prompt + rows
    far_rows = n_prompt // 2 - block
    width = HEADS_PER_STEP * rows
    lanes = 2 * HEAD_DIM
    shape = jax.ShapeDtypeStruct
    return pl.pallas_call(
        functools.partial(attention_kernel, len(blocks)),
        out_shape=[
            shape(queries.shape, BF16),
            shape(resp_keys.shape, BF16),
            shape(resp_keys.shape, BF16),
            shape((2 * block, lanes), BF16),
            shape((far_rows, lanes), BF16),
            shape((far_rows + RTILE, lanes), BF16),
            shape((RTILE, lanes), BF16),
        ],
        in_specs=[SMEM, SMEM] + [VMEM] * (5 + len(blocks)),
        out_specs=[VMEM] * 7,
        scratch_shapes=[
            pltpu.VMEM((n_keys, HEAD_DIM), BF16),
            pltpu.VMEM((n_keys, HEAD_DIM), BF16),
            pltpu.VMEM((HEAD_DIM, n_keys), BF16),
            pltpu.VMEM((n_keys, width), F32),
            pltpu.VMEM((n_keys, width), F32),
            pltpu.VMEM((n_keys, HEAD_DIM), F32),
            pltpu.VMEM((n_keys, HEAD_DIM), F32),
            pltpu.VMEM((1, queries.shape[1]), F32),
            pltpu.VMEM((1, queries.shape[1]), F32),
        ],
        compiler_params=pltpu.CompilerParams(vmem_limit_bytes=32 * 1024 * 1024),
        name="attention",
    )(pref_ids, resp_len, queries, out_grad, table, resp_keys, resp_values, *blocks)


def pair_sum_kernel(direct_ref, got_ref, r_ref, *out_refs):
    mate = got_ref[direct_ref.shape[0] :, :]
    at = 0
    for i, out in enumerate(out_refs):
        tiles = 1 if i == len(out_refs) - 1 else 2
        n = out.shape[0] - tiles * RTILE
        out[:n, :] = (
            direct_ref[at : at + n, :].astype(F32) + got_ref[at : at + n, :].astype(F32)
        ).astype(BF16)
        out[n : n + RTILE, :] = r_ref[...]
        if tiles == 2:
            out[n + RTILE :, :] = mate
        at += n


def pair_sum(direct, got, r_tile, block, near_count):
    lanes = direct.shape[1]
    shapes = [(2 * block + 2 * RTILE, lanes)] * near_count + [(block + RTILE, lanes)]
    return pl.pallas_call(
        pair_sum_kernel,
        out_shape=[jax.ShapeDtypeStruct(s, BF16) for s in shapes],
        in_specs=[VMEM] * 3,
        out_specs=[VMEM] * len(shapes),
        name="pair_sum",
    )(direct, got, r_tile)


def chip_sum_kernel(near_ref, *refs):
    block = near_ref.shape[0] // 2
    *got_refs, far_ref, mine_ref, other_ref = refs
    mine = near_ref[:block, :].astype(F32) + far_ref[:block, :].astype(F32)
    other = near_ref[block:, :].astype(F32)
    at = block
    for got in got_refs:
        mine = mine + got[:block, :].astype(F32)
        other = other + got[block : 2 * block, :].astype(F32)
        other_ref[at : at + 2 * RTILE, :] = got[2 * block :, :]
        at += 2 * RTILE
    other_ref[at:, :] = far_ref[block:, :]
    mine_ref[...] = mine
    other_ref[:block, :] = other.astype(BF16)


def chip_sum(near, gots, far):
    block, lanes = near.shape[0] // 2, near.shape[1]
    tiles = 2 * len(gots) + 1
    return pl.pallas_call(
        chip_sum_kernel,
        out_shape=[
            jax.ShapeDtypeStruct((block, lanes), F32),
            jax.ShapeDtypeStruct((block + tiles * RTILE, lanes), BF16),
        ],
        in_specs=[VMEM] * (len(gots) + 2),
        out_specs=[VMEM] * 2,
        name="chip_sum",
    )(near, *gots, far)


def last_sum_kernel(mine_ref, sent_ref, got_ref, r_ref, mate_ref, dk_ref, dv_ref, pref_ref):
    block = mine_ref.shape[0]
    total = mine_ref[...] + got_ref[:block, :].astype(F32)
    dk_ref[...] = total[:, :HEAD_DIM].astype(BF16)
    dv_ref[...] = total[:, HEAD_DIM:].astype(BF16)
    n_pref, columns = pref_ref.shape
    lanes = mine_ref.shape[1]
    tiles = [r_ref[...], mate_ref[...]]
    for ref in (sent_ref, got_ref):
        for at in range(block, ref.shape[0], RTILE):
            tiles.append(ref[at : at + RTILE, :])
    tiles = [t.astype(F32) for t in tiles]
    count = columns // lanes
    hot = jnp.concatenate([t[count : count + 1, :n_pref] for t in tiles], axis=0)
    hot = hot.astype(BF16)
    for j in range(count):
        sums = jnp.concatenate([t[j : j + 1, :] for t in tiles], axis=0).astype(BF16)
        pref_ref[:, j * lanes : (j + 1) * lanes] = lax.dot_general(
            hot, sums, (((0,), (0,)), ((), ())), preferred_element_type=F32
        )


def last_sum(mine, sent, got, r_tile, mate_tile, n_pref, columns):
    block = mine.shape[0]
    return pl.pallas_call(
        last_sum_kernel,
        out_shape=[
            jax.ShapeDtypeStruct((block, HEAD_DIM), BF16),
            jax.ShapeDtypeStruct((block, HEAD_DIM), BF16),
            jax.ShapeDtypeStruct((n_pref, columns), F32),
        ],
        in_specs=[VMEM] * 5,
        out_specs=[VMEM] * 3,
        name="last_sum",
    )(mine, sent, got, r_tile, mate_tile)


def shards(
    n_resp,
    queries,
    resp_keys,
    resp_values,
    prompt_keys,
    prompt_values,
    out_grad,
    pref_table,
    pref_ids,
    resp_len,
):
    pair, far, out, back = ring_moves(n_resp)

    def move(array, moves):
        return lax.ppermute(array, "resp", moves)

    block = prompt_keys.shape[0]
    own = jnp.concatenate([prompt_keys, prompt_values], axis=1)
    far_direct = move(own, far)
    chip = jnp.concatenate([own, move(own, pair)], axis=0)
    direct = [move(chip, moves) for moves in out] + [far_direct]
    via = [move(piece, pair) for piece in direct]
    query_grad, resp_key_grad, resp_value_grad, near, direct_sum, via_sum, r_tile = attention(
        pref_ids,
        resp_len,
        queries,
        out_grad,
        pref_table,
        resp_keys,
        resp_values,
        [chip] + direct + via,
    )
    got = move(via_sum, pair)
    *near_sums, far_sum = pair_sum(direct_sum, got, r_tile, block, len(out))
    far_got = move(far_sum, far)
    gots = [move(piece, moves) for piece, moves in zip(near_sums, back)]
    mine, sent = chip_sum(near, gots, far_got)
    last = move(sent, pair)
    prompt_key_grad, prompt_value_grad, pref_grad = last_sum(
        mine, sent, last, r_tile, got[-RTILE:], pref_table.shape[0], queries.shape[1]
    )
    return (
        query_grad,
        resp_key_grad,
        resp_value_grad,
        prompt_key_grad,
        prompt_value_grad,
        pref_grad,
    )


def solution(mesh):
    rows = P(("dp", "resp"), "tensor")
    in_specs = (rows,) * 6 + (P(None, "tensor"), P(("dp", "resp")), P(("dp", "resp")))
    out_specs = (rows,) * 5 + (P("dp", "tensor"),)
    return jax.shard_map(
        functools.partial(shards, mesh.shape["resp"]),
        mesh=mesh,
        in_specs=in_specs,
        out_specs=out_specs,
        check_vma=False,
    )
```

```python
import functools

import jax
import jax.numpy as jnp
from jax import lax
from jax.experimental import pallas as pl
from jax.experimental.pallas import tpu as pltpu
from jax.sharding import PartitionSpec as P

F32 = jnp.float32
BF16 = jnp.bfloat16
HEAD_DIM = 128
SCALING = HEAD_DIM**-0.5
LOG2E = 1.4426950408889634
HEADS_PER_STEP = 2
CHUNK = 256
RTILE = 16
NT = (((1,), (1,)), ((), ()))
NN = (((1,), (0,)), ((), ()))
VMEM = pl.BlockSpec(memory_space=pltpu.VMEM)
SMEM = pl.BlockSpec(memory_space=pltpu.SMEM)
ANY = pl.BlockSpec(memory_space=pltpu.HBM)
SMALL = pltpu.CompilerParams(vmem_limit_bytes=8 * 1024 * 1024)


def ring_moves(n_resp):
    chips = n_resp // 2
    places = [(chip, core) for chip in range(chips) for core in range(2)]

    def along(step):
        return [
            (z * 2 + c, (z + step if c == 0 else z - step) % chips * 2 + c) for z, c in places
        ]

    pair = [(z * 2 + c, z * 2 + 1 - c) for z, c in places]
    return pair, along


def columns_of(ref, group):
    parts = []
    for i in range(HEADS_PER_STEP):
        at = (group * HEADS_PER_STEP + i) * HEAD_DIM
        parts.append(ref[:, at : at + HEAD_DIM])
    return jnp.concatenate(parts, axis=0)


def scores_kernel(n_blocks, has_resp, q_ref, g_ref, *refs):
    block_refs = refs[:n_blocks]
    resp_refs = refs[n_blocks : n_blocks + 2 * has_resp]
    low_ref, dp_ref, stat_ref, keys_t_ref, *score_refs = refs[n_blocks + 2 * has_resp :]
    rows = q_ref.shape[0]
    width = HEADS_PER_STEP * rows
    factor = SCALING * LOG2E
    pieces = []
    at = 0
    for ref in block_refs:
        n = ref.shape[0]
        pieces.append((at, n, ref.at[:, :HEAD_DIM], ref.at[:, HEAD_DIM:], False))
        at += n
    if has_resp:
        pieces.append((at, rows, resp_refs[0], resp_refs[1], True))
    for at, n, key_ref, _, _ in pieces:
        keys_t_ref[:, at : at + n] = key_ref[...].T
    for group in range(q_ref.shape[1] // (HEADS_PER_STEP * HEAD_DIM)):
        s_scr = score_refs[group % 2]
        cols = slice(group * width, (group + 1) * width)
        q = columns_of(q_ref, group)
        g = columns_of(g_ref, group)
        top = jnp.full((8, width), -1e30, F32)
        for at, n, key_ref, _, is_resp in pieces:
            s = lax.dot_general(key_ref[...], q, NT, preferred_element_type=F32)
            if is_resp:
                key_pos = lax.broadcasted_iota(jnp.int32, (n, width), 0)
                query_pos = lax.broadcasted_iota(jnp.int32, (n, width), 1) % rows
                s = jnp.where(key_pos <= query_pos, s, -1e30)
            s_scr[at : at + n, :] = s
            top = jnp.maximum(top, jnp.max(s.reshape(n // 8, 8, width), axis=0))
        row_max = jnp.max(top, axis=0, keepdims=True) * factor
        total = jnp.zeros((8, width), F32)
        dot = jnp.zeros((8, width), F32)
        for at, n, _, value_ref, _ in pieces:
            p = jnp.exp2(s_scr[at : at + n, :] * factor - row_max)
            dp = lax.dot_general(value_ref[...], g, NT, preferred_element_type=F32)
            total = total + jnp.sum(p.reshape(n // 8, 8, width), axis=0)
            dot = dot + jnp.sum((p * dp).reshape(n // 8, 8, width), axis=0)
            low_ref[at : at + n, cols] = p.astype(BF16)
            dp_ref[at : at + n, cols] = dp
        stat_ref[0:1, cols] = row_max
        stat_ref[1:2, cols] = jnp.sum(total, axis=0, keepdims=True)
        stat_ref[2:3, cols] = jnp.sum(dot, axis=0, keepdims=True)


def scores(biased, masked, blocks, resp=()):
    rows, columns = biased.shape
    n = sum(b.shape[0] for b in blocks) + (rows if resp else 0)
    queries = rows * columns // HEAD_DIM
    shape = jax.ShapeDtypeStruct
    return pl.pallas_call(
        functools.partial(scores_kernel, len(blocks), bool(resp)),
        out_shape=[
            shape((n, queries), BF16),
            shape((n, queries), F32),
            shape((8, queries), F32),
            shape((HEAD_DIM, n), BF16),
        ],
        in_specs=[VMEM] * (2 + len(blocks) + len(resp)),
        out_specs=[VMEM] * 4,
        scratch_shapes=[pltpu.VMEM((n, HEADS_PER_STEP * rows), F32)] * 2,
        compiler_params=SMALL,
        cost_estimate=pl.CostEstimate(
            flops=4 * n * queries * HEAD_DIM, bytes_accessed=0, transcendentals=n * queries
        ),
        name="scores",
    )(biased, masked, *blocks, *resp)


def query_kernel(count, id_ref, *refs):
    low_refs = refs[:count]
    dp_refs = refs[count : 2 * count]
    stat_refs = refs[2 * count : 3 * count]
    key_refs = refs[3 * count : 4 * count]
    ds_refs = refs[4 * count : 5 * count]
    dq_ref, scale_ref, r_ref, sum_scr, delta_scr = refs[5 * count :]
    rows, columns = dq_ref.shape
    width = HEADS_PER_STEP * rows
    top = stat_refs[0][0:1, :]
    for ref in stat_refs[1:]:
        top = jnp.maximum(top, ref[0:1, :])
    total = dot = 0.0
    for i, ref in enumerate(stat_refs):
        shift = jnp.exp2(ref[0:1, :] - top)
        scale_ref[i : i + 1, :] = shift
        total = total + ref[1:2, :] * shift
        dot = dot + ref[2:3, :] * shift
    inverse = 1.0 / total
    delta_scr[...] = dot * inverse
    for i in range(count):
        scale_ref[i : i + 1, :] = scale_ref[i : i + 1, :] * inverse
    for group in range(columns // (HEADS_PER_STEP * HEAD_DIM)):
        cols = slice(group * width, (group + 1) * width)
        delta = delta_scr[:, cols]
        dq = jnp.zeros((HEAD_DIM, width), F32)
        for i in range(count):
            ds = low_refs[i][:, cols] * (dp_refs[i][:, cols] - delta).astype(BF16)
            ds_refs[i][:, cols] = ds
            part = lax.dot_general(key_refs[i][...], ds, NN, preferred_element_type=F32)
            dq = dq + part * scale_ref[i : i + 1, cols]
        dq = dq.T * SCALING
        for i in range(HEADS_PER_STEP):
            at = (group * HEADS_PER_STEP + i) * HEAD_DIM
            part = dq[i * rows : (i + 1) * rows]
            dq_ref[:, at : at + HEAD_DIM] = part.astype(BF16)
            sum_scr[:, at : at + HEAD_DIM] = jnp.sum(part, axis=0, keepdims=True)
    lanes = 2 * HEAD_DIM
    pieces = [sum_scr[:, j * lanes : (j + 1) * lanes] for j in range(columns // lanes)]
    hot = (lax.broadcasted_iota(jnp.int32, (1, lanes), 1) == id_ref[0]).astype(F32)
    blank = jnp.zeros((RTILE - columns // lanes - 1, lanes), F32)
    r_ref[...] = jnp.concatenate(pieces + [hot, blank], axis=0).astype(BF16)


def query_side(pref_ids, lows, dps, stats, keys_t, rows, columns):
    count = len(lows)
    queries = lows[0].shape[1]
    shape = jax.ShapeDtypeStruct
    keys = sum(low.shape[0] for low in lows)
    return pl.pallas_call(
        functools.partial(query_kernel, count),
        out_shape=[shape(low.shape, BF16) for low in lows]
        + [
            shape((rows, columns), BF16),
            shape((8, queries), F32),
            shape((RTILE, 2 * HEAD_DIM), BF16),
        ],
        in_specs=[SMEM] + [VMEM] * (4 * count),
        out_specs=[VMEM] * (count + 3),
        scratch_shapes=[pltpu.VMEM((1, columns), F32), pltpu.VMEM((1, queries), F32)],
        compiler_params=SMALL,
        cost_estimate=pl.CostEstimate(
            flops=2 * keys * queries * HEAD_DIM, bytes_accessed=0, transcendentals=0
        ),
        name="query_side",
    )(pref_ids, *lows, *dps, *stats, *keys_t)


def key_kernel(picks, has_r, scale_ref, q_ref, g_ref, *refs):
    count = len(picks)
    ds_refs = refs[:count]
    low_refs = refs[count : 2 * count]
    r_refs = refs[2 * count : 2 * count + has_r]
    *out_refs, q_scr, g_scr = refs[2 * count + has_r :]
    rows = q_ref.shape[0]
    results = []
    for i, pick in enumerate(picks):
        for head in range(q_ref.shape[1] // HEAD_DIM):
            at = slice(head * rows, (head + 1) * rows)
            cols = slice(head * HEAD_DIM, (head + 1) * HEAD_DIM)
            scale = jnp.broadcast_to(scale_ref[pick : pick + 1, at], (HEAD_DIM, rows)).T
            q_scr[i, at, :] = (q_ref[:, cols].astype(F32) * scale).astype(BF16)
            g_scr[i, at, :] = (g_ref[:, cols].astype(F32) * scale).astype(BF16)
        dk = lax.dot_general(ds_refs[i][...], q_scr[i], NN, preferred_element_type=F32) * SCALING
        dv = lax.dot_general(low_refs[i][...], g_scr[i], NN, preferred_element_type=F32)
        results.append((dk.astype(BF16), dv.astype(BF16)))
    if has_r or count > 1:
        for ref, (dk, dv) in zip(out_refs, results):
            n = dk.shape[0]
            ref[:n, :HEAD_DIM] = dk
            ref[:n, HEAD_DIM:] = dv
        if has_r:
            out_refs[-1][n:, :] = r_refs[0][...]
    else:
        near_ref, drk_ref, drv_ref = out_refs
        n = near_ref.shape[0]
        dk, dv = results[0]
        near_ref[:, :HEAD_DIM] = dk[:n, :]
        near_ref[:, HEAD_DIM:] = dv[:n, :]
        drk_ref[...] = dk[n:, :]
        drv_ref[...] = dv[n:, :]


def key_side(picks, scale, biased, masked, ds, lows, r_tile=()):
    rows, columns = biased.shape
    queries = rows * columns // HEAD_DIM
    lanes = 2 * HEAD_DIM
    if len(picks) > 1:
        counts = [d.shape[0] for d in ds]
        counts[-1] += RTILE * len(r_tile)
        shapes = [(n, lanes) for n in counts]
    else:
        shapes = [(ds[0].shape[0] - rows, lanes), (rows, HEAD_DIM), (rows, HEAD_DIM)]
    keys = sum(d.shape[0] for d in ds)
    return pl.pallas_call(
        functools.partial(key_kernel, picks, len(r_tile)),
        out_shape=[jax.ShapeDtypeStruct(s, BF16) for s in shapes],
        in_specs=[VMEM] * (3 + 2 * len(picks) + len(r_tile)),
        out_specs=[VMEM] * len(shapes),
        scratch_shapes=[pltpu.VMEM((len(picks), queries, HEAD_DIM), BF16)] * 2,
        compiler_params=SMALL,
        cost_estimate=pl.CostEstimate(
            flops=4 * keys * queries * HEAD_DIM, bytes_accessed=0, transcendentals=0
        ),
        name="key_side",
    )(scale, biased, masked, *ds, *lows, *r_tile)


def pack_kernel(k_ref, v_ref, own_ref, sems):
    copies = [
        pltpu.make_async_copy(k_ref, own_ref.at[:, :HEAD_DIM], sems.at[0]),
        pltpu.make_async_copy(v_ref, own_ref.at[:, HEAD_DIM:], sems.at[1]),
    ]
    for copy in copies:
        copy.start()
    for copy in copies:
        copy.wait()


def pack(keys, values):
    return pl.pallas_call(
        pack_kernel,
        out_shape=jax.ShapeDtypeStruct((keys.shape[0], 2 * HEAD_DIM), BF16),
        in_specs=[ANY, ANY],
        out_specs=VMEM,
        scratch_shapes=[pltpu.SemaphoreType.DMA((2,))],
        compiler_params=SMALL,
        name="pack",
    )(keys, values)


def prepare_kernel(
    id_ref,
    len_ref,
    q_hbm,
    g_hbm,
    table_hbm,
    rk_hbm,
    rv_hbm,
    biased_ref,
    masked_ref,
    rk_ref,
    rv_ref,
    table_ref,
    sems,
):
    arrays = [
        (table_hbm, table_ref),
        (q_hbm, biased_ref),
        (g_hbm, masked_ref),
        (rk_hbm, rk_ref),
        (rv_hbm, rv_ref),
    ]
    copies = [pltpu.make_async_copy(a, b, sems.at[i]) for i, (a, b) in enumerate(arrays)]
    for copy in copies:
        copy.start()
    copies[0].wait()
    chosen = lax.broadcasted_iota(jnp.int32, table_ref.shape, 0) == id_ref[0]
    pref = jnp.sum(jnp.where(chosen, table_ref[...].astype(F32), 0.0), axis=0, keepdims=True)
    copies[1].wait()
    biased_ref[...] = (biased_ref[...].astype(F32) + pref).astype(BF16)
    copies[2].wait()
    live = lax.broadcasted_iota(jnp.int32, masked_ref.shape, 0) < len_ref[0]
    masked_ref[...] = jnp.where(live, masked_ref[...], jnp.zeros((), BF16))
    copies[3].wait()
    copies[4].wait()


def prepare(pref_ids, resp_len, queries, out_grad, table, resp_keys, resp_values):
    wide = jax.ShapeDtypeStruct(queries.shape, BF16)
    slim = jax.ShapeDtypeStruct(resp_keys.shape, BF16)
    return pl.pallas_call(
        prepare_kernel,
        out_shape=[wide, wide, slim, slim],
        in_specs=[SMEM, SMEM] + [ANY] * 5,
        out_specs=[VMEM] * 4,
        scratch_shapes=[pltpu.VMEM(table.shape, BF16), pltpu.SemaphoreType.DMA((5,))],
        compiler_params=SMALL,
        cost_estimate=pl.CostEstimate(
            flops=4 * queries.size, bytes_accessed=8 * queries.size, transcendentals=0
        ),
        name="prepare",
    )(pref_ids, resp_len, queries, out_grad, table, resp_keys, resp_values)


def pair_sum_kernel(tiles, direct_ref, got_ref, r_ref, mate_ref, *out_refs):
    at = 0
    for out, count in zip(out_refs, tiles):
        n = out.shape[0] - count * RTILE
        total = direct_ref[at : at + n, :].astype(F32) + got_ref[at : at + n, :].astype(F32)
        out[:n, :] = total.astype(out.dtype)
        if count:
            out[n : n + RTILE, :] = r_ref[...]
        if count == 2:
            out[n + RTILE :, :] = mate_ref[mate_ref.shape[0] - RTILE :, :]
        at += n


def pair_sum(direct, got, r_tile, mate, sizes, tiles):
    lanes = direct.shape[1]
    return pl.pallas_call(
        functools.partial(pair_sum_kernel, tiles),
        out_shape=[
            jax.ShapeDtypeStruct((n + t * RTILE, lanes), BF16 if t else F32)
            for n, t in zip(sizes, tiles)
        ],
        in_specs=[VMEM] * 4,
        out_specs=[VMEM] * len(sizes),
        compiler_params=SMALL,
        name="pair_sum",
    )(direct, got, r_tile, mate)


def middle_sum_kernel(two_ref, three_ref, four_ref, r_ref, got_ref, out_ref):
    rows = two_ref.shape[0]
    block = rows // 2
    total = two_ref[...] + three_ref[:rows, :].astype(F32)
    out_ref[:block, :] = (total[:block, :] + four_ref[:block, :].astype(F32)).astype(BF16)
    out_ref[block:rows, :] = total[block:, :].astype(BF16)
    out_ref[rows : rows + RTILE, :] = r_ref[...]
    out_ref[rows + RTILE : rows + 2 * RTILE, :] = got_ref[got_ref.shape[0] - RTILE :, :]
    out_ref[rows + 2 * RTILE : rows + 4 * RTILE, :] = three_ref[rows:, :]
    out_ref[rows + 4 * RTILE :, :] = four_ref[block:, :]


def middle_sum(two, three, four, r_tile, got):
    return pl.pallas_call(
        middle_sum_kernel,
        out_shape=jax.ShapeDtypeStruct((two.shape[0] + 5 * RTILE, two.shape[1]), BF16),
        in_specs=[VMEM] * 5,
        out_specs=VMEM,
        compiler_params=SMALL,
        name="middle_sum",
    )(two, three, four, r_tile, got)


def chip_sum_kernel(near_ref, one_ref, two_ref, mine_ref, other_ref):
    rows = near_ref.shape[0]
    block = rows // 2
    total = near_ref[...].astype(F32) + one_ref[:rows, :].astype(F32) + two_ref[:rows, :].astype(F32)
    mine_ref[...] = total[:block, :]
    other_ref[:block, :] = total[block:, :].astype(BF16)
    split = block + one_ref.shape[0] - rows
    other_ref[block:split, :] = one_ref[rows:, :]
    other_ref[split:, :] = two_ref[rows:, :]


def chip_sum(near, one, two):
    rows, lanes = near.shape
    block = rows // 2
    sent = block + one.shape[0] + two.shape[0] - 2 * rows
    return pl.pallas_call(
        chip_sum_kernel,
        out_shape=[
            jax.ShapeDtypeStruct((block, lanes), F32),
            jax.ShapeDtypeStruct((sent, lanes), BF16),
        ],
        in_specs=[VMEM] * 3,
        out_specs=[VMEM] * 2,
        compiler_params=SMALL,
        name="chip_sum",
    )(near, one, two)


def last_sum_kernel(mine_ref, sent_ref, last_ref, r_ref, got_ref, dk_ref, dv_ref, pref_ref):
    block = mine_ref.shape[0]
    total = mine_ref[...] + last_ref[:block, :].astype(F32)
    dk_ref[...] = total[:, :HEAD_DIM].astype(BF16)
    dv_ref[...] = total[:, HEAD_DIM:].astype(BF16)
    n_pref, columns = pref_ref.shape
    lanes = mine_ref.shape[1]
    tiles = [r_ref[...], got_ref[got_ref.shape[0] - RTILE :, :]]
    for ref in (sent_ref, last_ref):
        for at in range(block, ref.shape[0], RTILE):
            tiles.append(ref[at : at + RTILE, :])
    tiles = [t.astype(F32) for t in tiles]
    count = columns // lanes
    hot = jnp.concatenate([t[count : count + 1, :n_pref] for t in tiles], axis=0)
    hot = hot.astype(BF16)
    for j in range(count):
        sums = jnp.concatenate([t[j : j + 1, :] for t in tiles], axis=0).astype(BF16)
        pref_ref[:, j * lanes : (j + 1) * lanes] = lax.dot_general(
            hot, sums, (((0,), (0,)), ((), ())), preferred_element_type=F32
        )


def last_sum(mine, sent, last, r_tile, got, n_pref, columns):
    block = mine.shape[0]
    return pl.pallas_call(
        last_sum_kernel,
        out_shape=[
            jax.ShapeDtypeStruct((block, HEAD_DIM), BF16),
            jax.ShapeDtypeStruct((block, HEAD_DIM), BF16),
            jax.ShapeDtypeStruct((n_pref, columns), F32),
        ],
        in_specs=[VMEM] * 5,
        out_specs=[VMEM] * 3,
        compiler_params=SMALL,
        name="last_sum",
    )(mine, sent, last, r_tile, got)


def in_hbm(array):
    return pltpu.with_memory_space_constraint(array, pltpu.HBM)


def shards(
    n_resp,
    queries,
    resp_keys,
    resp_values,
    prompt_keys,
    prompt_values,
    out_grad,
    pref_table,
    pref_ids,
    resp_len,
):
    pair, along = ring_moves(n_resp)

    def move(array, moves):
        return lax.ppermute(array, "resp", moves)

    block = prompt_keys.shape[0]
    arrays = (queries, out_grad, pref_table, resp_keys, resp_values)
    biased, masked, resp_keys, resp_values = prepare(
        pref_ids, resp_len, *[in_hbm(array) for array in arrays]
    )
    own = pack(in_hbm(prompt_keys), in_hbm(prompt_values))
    chip = jnp.concatenate([own, move(own, pair)], axis=0)
    chip, biased, masked = lax.optimization_barrier((chip, biased, masked))
    second = move(chip, along(2))
    first = move(chip, along(1))
    part0 = scores(biased, masked, [chip], (resp_keys, resp_values))
    second, part0 = lax.optimization_barrier((second, part0))
    third = move(second, along(1))
    fourth = move(second[:block], along(2))
    part1 = scores(biased, masked, [first, second])
    part2 = scores(biased, masked, [move(first, pair), move(second, pair)])
    third, fourth, part1, part2 = lax.optimization_barrier((third, fourth, part1, part2))
    part3 = scores(biased, masked, [third, fourth])
    part4 = scores(biased, masked, [move(third, pair), move(fourth, pair)])
    parts = [part0, part1, part2, part3, part4]
    lows, dps, stats, keys_t = zip(*parts)
    *ds, query_grad, scale, r_tile = query_side(
        pref_ids, lows, dps, stats, keys_t, queries.shape[0], queries.shape[1]
    )

    def keys_of(picks, *tile):
        return key_side(
            picks, scale, biased, masked, [ds[i] for i in picks], [lows[i] for i in picks], tile
        )

    direct_far, via_far = keys_of((3, 4), r_tile)
    got = move(via_far, pair)
    three, four = pair_sum(direct_far, got, r_tile, got, (2 * block, block), (2, 1))
    direct_close, via_close = keys_of((1, 2))
    one, two = pair_sum(
        direct_close, move(via_close, pair), r_tile, got, (2 * block, 2 * block), (2, 0)
    )
    near, resp_key_grad, resp_value_grad = keys_of((0,))
    four = move(four, along(-2))
    three = move(three, along(-1))
    one = move(one, along(-1))
    two = move(middle_sum(two, three, four, r_tile, got), along(-2))
    mine, sent = chip_sum(near, one, two)
    last = move(sent, pair)
    prompt_key_grad, prompt_value_grad, pref_grad = last_sum(
        mine, sent, last, r_tile, got, pref_table.shape[0], queries.shape[1]
    )
    return (
        query_grad,
        resp_key_grad,
        resp_value_grad,
        prompt_key_grad,
        prompt_value_grad,
        pref_grad,
    )


def solution(mesh):
    rows = P(("dp", "resp"), "tensor")
    in_specs = (rows,) * 6 + (P(None, "tensor"), P(("dp", "resp")), P(("dp", "resp")))
    out_specs = (rows,) * 5 + (P("dp", "tensor"),)
    return jax.shard_map(
        functools.partial(shards, mesh.shape["resp"]),
        mesh=mesh,
        in_specs=in_specs,
        out_specs=out_specs,
        check_vma=False,
    )
```

```python
import functools

import jax
import jax.numpy as jnp
from jax import lax
from jax.experimental import pallas as pl
from jax.experimental.pallas import tpu as pltpu
from jax.sharding import PartitionSpec as P

F32 = jnp.float32
BF16 = jnp.bfloat16
HEAD_DIM = 128
SCALING = HEAD_DIM**-0.5
LOG2E = 1.4426950408889634
HEADS_PER_STEP = 2
CHUNK = 256
RTILE = 16
NT = (((1,), (1,)), ((), ()))
NN = (((1,), (0,)), ((), ()))
VMEM = pl.BlockSpec(memory_space=pltpu.VMEM)
SMEM = pl.BlockSpec(memory_space=pltpu.SMEM)
ANY = pl.BlockSpec(memory_space=pltpu.HBM)
SMALL = pltpu.CompilerParams(vmem_limit_bytes=8 * 1024 * 1024)


def ring_moves(n_resp):
    chips = n_resp // 2
    places = [(chip, core) for chip in range(chips) for core in range(2)]

    def index(chip, core):
        return chip % chips * 2 + core

    def sign(chip, core, period):
        return 1 if (chip % period < period // 2) == (core == 0) else -1

    def reply_core(chip, neighbour):
        return 0 if sign(neighbour, 0, 4) == neighbour - chip else 1

    pair, one, two, three, four = [], [], [], [], []
    for z, c in places:
        me = index(z, c)
        pair.append((me, index(z, 1 - c)))
        one.append((me, index(z + sign(z, c, 2), c)))
        step = sign(z, c, 4)
        two.append((me, index(z + 2 * step, c)))
        three.append((me, index(z - step, reply_core(z, z - step))))
        four.append((me, index(z - 2 * step, c)))
    for moves in (pair, one, two, three, four):
        assert sorted(moves) == sorted((b, a) for a, b in moves)
    return pair, one, two, three, four


def scores_kernel(n_blocks, has_resp, q_ref, g_ref, *refs):
    block_refs = refs[:n_blocks]
    resp_refs = refs[n_blocks : n_blocks + 2 * has_resp]
    low_ref, dp_ref, stat_ref, keys_t_ref, *score_refs = refs[n_blocks + 2 * has_resp :]
    rows = q_ref.shape[0]
    factor = SCALING * LOG2E
    pieces = []
    at = 0
    for ref in block_refs:
        n = ref.shape[0]
        pieces.append((at, n, ref.at[:, :HEAD_DIM], ref.at[:, HEAD_DIM:], False))
        at += n
    if has_resp:
        pieces.append((at, rows, resp_refs[0], resp_refs[1], True))
    for at, n, key_ref, _, _ in pieces:
        keys_t_ref[:, at : at + n] = key_ref[...].T

    def score(head, piece, top):
        at, n, key_ref, _, is_resp = piece
        q = q_ref[:, head * HEAD_DIM : (head + 1) * HEAD_DIM]
        s = lax.dot_general(key_ref[...], q, NT, preferred_element_type=F32)
        if is_resp:
            key_pos = lax.broadcasted_iota(jnp.int32, (n, rows), 0)
            query_pos = lax.broadcasted_iota(jnp.int32, (n, rows), 1)
            s = jnp.where(key_pos <= query_pos, s, -1e30)
        score_refs[head % 2][at : at + n, :] = s
        return jnp.maximum(top, jnp.max(s.reshape(n // 8, 8, rows), axis=0))

    lowest = jnp.full((8, rows), -1e30, F32)
    heads = q_ref.shape[1] // HEAD_DIM
    top = lowest
    for piece in pieces:
        top = score(0, piece, top)
    for head in range(heads):
        cols = slice(head * rows, (head + 1) * rows)
        g = g_ref[:, head * HEAD_DIM : (head + 1) * HEAD_DIM]
        row_max = jnp.max(top, axis=0, keepdims=True) * factor
        total = jnp.zeros((8, rows), F32)
        dot = jnp.zeros((8, rows), F32)
        top = lowest
        for piece in pieces:
            at, n, _, value_ref, _ = piece
            p = jnp.exp2(score_refs[head % 2][at : at + n, :] * factor - row_max)
            dp = lax.dot_general(value_ref[...], g, NT, preferred_element_type=F32)
            total = total + jnp.sum(p.reshape(n // 8, 8, rows), axis=0)
            dot = dot + jnp.sum((p * dp).reshape(n // 8, 8, rows), axis=0)
            low_ref[at : at + n, cols] = p.astype(BF16)
            dp_ref[at : at + n, cols] = dp
            if head + 1 < heads:
                top = score(head + 1, piece, top)
        stat_ref[0:1, cols] = row_max
        stat_ref[1:2, cols] = jnp.sum(total, axis=0, keepdims=True)
        stat_ref[2:3, cols] = jnp.sum(dot, axis=0, keepdims=True)


def scores(biased, masked, blocks, resp=()):
    rows, columns = biased.shape
    n = sum(b.shape[0] for b in blocks) + (rows if resp else 0)
    queries = rows * columns // HEAD_DIM
    shape = jax.ShapeDtypeStruct
    return pl.pallas_call(
        functools.partial(scores_kernel, len(blocks), bool(resp)),
        out_shape=[
            shape((n, queries), BF16),
            shape((n, queries), F32),
            shape((8, queries), F32),
            shape((HEAD_DIM, n), BF16),
        ],
        in_specs=[VMEM] * (2 + len(blocks) + len(resp)),
        out_specs=[VMEM] * 4,
        scratch_shapes=[pltpu.VMEM((n, rows), F32)] * 2,
        compiler_params=SMALL,
        cost_estimate=pl.CostEstimate(
            flops=4 * n * queries * HEAD_DIM, bytes_accessed=0, transcendentals=n * queries
        ),
        name="scores",
    )(biased, masked, *blocks, *resp)


def query_kernel(count, id_ref, *refs):
    low_refs = refs[:count]
    dp_refs = refs[count : 2 * count]
    stat_refs = refs[2 * count : 3 * count]
    key_refs = refs[3 * count : 4 * count]
    ds_refs = refs[4 * count : 5 * count]
    dq_ref, scale_ref, r_ref, sum_scr, delta_scr = refs[5 * count :]
    rows, columns = dq_ref.shape
    width = HEADS_PER_STEP * rows
    top = stat_refs[0][0:1, :]
    for ref in stat_refs[1:]:
        top = jnp.maximum(top, ref[0:1, :])
    total = dot = 0.0
    for i, ref in enumerate(stat_refs):
        shift = jnp.exp2(ref[0:1, :] - top)
        scale_ref[i : i + 1, :] = shift
        total = total + ref[1:2, :] * shift
        dot = dot + ref[2:3, :] * shift
    inverse = 1.0 / total
    delta_scr[...] = dot * inverse
    for i in range(count):
        scale_ref[i : i + 1, :] = scale_ref[i : i + 1, :] * inverse
    for group in range(columns // (HEADS_PER_STEP * HEAD_DIM)):
        cols = slice(group * width, (group + 1) * width)
        delta = delta_scr[:, cols]
        dq = jnp.zeros((HEAD_DIM, width), F32)
        for i in range(count):
            ds = low_refs[i][:, cols] * (dp_refs[i][:, cols] - delta).astype(BF16)
            ds_refs[i][:, cols] = ds
            part = lax.dot_general(key_refs[i][...], ds, NN, preferred_element_type=F32)
            dq = dq + part * scale_ref[i : i + 1, cols]
        dq = dq.T * SCALING
        for i in range(HEADS_PER_STEP):
            at = (group * HEADS_PER_STEP + i) * HEAD_DIM
            part = dq[i * rows : (i + 1) * rows]
            dq_ref[:, at : at + HEAD_DIM] = part.astype(BF16)
            sum_scr[:, at : at + HEAD_DIM] = jnp.sum(part, axis=0, keepdims=True)
    lanes = 2 * HEAD_DIM
    pieces = [sum_scr[:, j * lanes : (j + 1) * lanes] for j in range(columns // lanes)]
    hot = (lax.broadcasted_iota(jnp.int32, (1, lanes), 1) == id_ref[0]).astype(F32)
    blank = jnp.zeros((RTILE - columns // lanes - 1, lanes), F32)
    r_ref[...] = jnp.concatenate(pieces + [hot, blank], axis=0).astype(BF16)


def query_side(pref_ids, lows, dps, stats, keys_t, rows, columns):
    count = len(lows)
    queries = lows[0].shape[1]
    shape = jax.ShapeDtypeStruct
    keys = sum(low.shape[0] for low in lows)
    return pl.pallas_call(
        functools.partial(query_kernel, count),
        out_shape=[shape(low.shape, BF16) for low in lows]
        + [
            shape((rows, columns), BF16),
            shape((8, queries), F32),
            shape((RTILE, 2 * HEAD_DIM), BF16),
        ],
        in_specs=[SMEM] + [VMEM] * (4 * count),
        out_specs=[VMEM] * (count + 3),
        scratch_shapes=[pltpu.VMEM((1, columns), F32), pltpu.VMEM((1, queries), F32)],
        compiler_params=SMALL,
        cost_estimate=pl.CostEstimate(
            flops=2 * keys * queries * HEAD_DIM, bytes_accessed=0, transcendentals=0
        ),
        name="query_side",
    )(pref_ids, *lows, *dps, *stats, *keys_t)


def key_kernel(picks, extra, scale_ref, q_ref, g_ref, *refs):
    count = len(picks)
    ds_refs = refs[:count]
    low_refs = refs[count : 2 * count]
    extra_refs = refs[2 * count : 2 * count + extra]
    *out_refs, q_scr, g_scr, sem = refs[2 * count + extra :]
    is_near = len(out_refs) > 2
    if is_near:
        flush = pltpu.make_async_copy(extra_refs[0], out_refs[3], sem)
        flush.start()
    rows = q_ref.shape[0]
    results = []
    for i, pick in enumerate(picks):
        for head in range(q_ref.shape[1] // HEAD_DIM):
            at = slice(head * rows, (head + 1) * rows)
            cols = slice(head * HEAD_DIM, (head + 1) * HEAD_DIM)
            scale = jnp.broadcast_to(scale_ref[pick : pick + 1, at], (HEAD_DIM, rows)).T
            q_scr[i, at, :] = (q_ref[:, cols].astype(F32) * scale).astype(BF16)
            g_scr[i, at, :] = (g_ref[:, cols].astype(F32) * scale).astype(BF16)
        dk = lax.dot_general(ds_refs[i][...], q_scr[i], NN, preferred_element_type=F32) * SCALING
        dv = lax.dot_general(low_refs[i][...], g_scr[i], NN, preferred_element_type=F32)
        results.append((dk.astype(BF16), dv.astype(BF16)))
    if not is_near:
        for ref, (dk, dv) in zip(out_refs, results):
            n = dk.shape[0]
            ref[:n, :HEAD_DIM] = dk
            ref[:n, HEAD_DIM:] = dv
        if extra:
            out_refs[-1][n:, :] = extra_refs[0][...]
    else:
        near_ref, drk_ref, drv_ref, _ = out_refs
        n = near_ref.shape[0]
        dk, dv = results[0]
        near_ref[:, :HEAD_DIM] = dk[:n, :]
        near_ref[:, HEAD_DIM:] = dv[:n, :]
        drk_ref[...] = dk[n:, :]
        drv_ref[...] = dv[n:, :]
        flush.wait()


def key_side(picks, scale, biased, masked, ds, lows, near, extra):
    rows, columns = biased.shape
    queries = rows * columns // HEAD_DIM
    lanes = 2 * HEAD_DIM
    if not near:
        counts = [d.shape[0] for d in ds]
        counts[-1] += RTILE * len(extra)
        shapes = [(n, lanes) for n in counts]
    else:
        shapes = [(ds[0].shape[0] - rows, lanes), (rows, HEAD_DIM), (rows, HEAD_DIM)]
        shapes.append((rows, columns))
    keys = sum(d.shape[0] for d in ds)
    return pl.pallas_call(
        functools.partial(key_kernel, picks, len(extra)),
        out_shape=[jax.ShapeDtypeStruct(s, BF16) for s in shapes],
        in_specs=[VMEM] * (3 + 2 * len(picks) + len(extra)),
        out_specs=[VMEM] * 3 + [ANY] if near else [VMEM] * len(shapes),
        scratch_shapes=[pltpu.VMEM((len(picks), queries, HEAD_DIM), BF16)] * 2
        + [pltpu.SemaphoreType.DMA],
        compiler_params=SMALL,
        cost_estimate=pl.CostEstimate(
            flops=4 * keys * queries * HEAD_DIM, bytes_accessed=0, transcendentals=0
        ),
        name="key_side",
    )(scale, biased, masked, *ds, *lows, *extra)


def pack_kernel(k_ref, v_ref, own_ref, sems):
    copies = [
        pltpu.make_async_copy(k_ref, own_ref.at[:, :HEAD_DIM], sems.at[0]),
        pltpu.make_async_copy(v_ref, own_ref.at[:, HEAD_DIM:], sems.at[1]),
    ]
    for copy in copies:
        copy.start()
    for copy in copies:
        copy.wait()


def pack(keys, values):
    return pl.pallas_call(
        pack_kernel,
        out_shape=jax.ShapeDtypeStruct((keys.shape[0], 2 * HEAD_DIM), BF16),
        in_specs=[ANY, ANY],
        out_specs=VMEM,
        scratch_shapes=[pltpu.SemaphoreType.DMA((2,))],
        compiler_params=SMALL,
        name="pack",
    )(keys, values)


def assemble_kernel(own_ref, k_ref, v_ref, chip_ref):
    n = own_ref.shape[0]
    chip_ref[:n, :] = own_ref[...]
    chip_ref[n:, :HEAD_DIM] = k_ref[...]
    chip_ref[n:, HEAD_DIM:] = v_ref[...]


def assemble(own, keys, values):
    return pl.pallas_call(
        assemble_kernel,
        out_shape=jax.ShapeDtypeStruct((2 * own.shape[0], own.shape[1]), BF16),
        in_specs=[VMEM] * 3,
        out_specs=VMEM,
        compiler_params=SMALL,
        name="assemble",
    )(own, keys, values)


def prepare_kernel(
    id_ref,
    len_ref,
    q_hbm,
    g_hbm,
    table_hbm,
    rk_hbm,
    rv_hbm,
    biased_ref,
    masked_ref,
    rk_ref,
    rv_ref,
    table_ref,
    sems,
):
    arrays = [
        (table_hbm, table_ref),
        (q_hbm, biased_ref),
        (g_hbm, masked_ref),
        (rk_hbm, rk_ref),
        (rv_hbm, rv_ref),
    ]
    copies = [pltpu.make_async_copy(a, b, sems.at[i]) for i, (a, b) in enumerate(arrays)]
    for copy in copies:
        copy.start()
    copies[0].wait()
    chosen = lax.broadcasted_iota(jnp.int32, table_ref.shape, 0) == id_ref[0]
    pref = jnp.sum(jnp.where(chosen, table_ref[...].astype(F32), 0.0), axis=0, keepdims=True)
    copies[1].wait()
    biased_ref[...] = (biased_ref[...].astype(F32) + pref).astype(BF16)
    copies[2].wait()
    live = lax.broadcasted_iota(jnp.int32, masked_ref.shape, 0) < len_ref[0]
    masked_ref[...] = jnp.where(live, masked_ref[...], jnp.zeros((), BF16))
    copies[3].wait()
    copies[4].wait()


def prepare(pref_ids, resp_len, queries, out_grad, table, resp_keys, resp_values):
    wide = jax.ShapeDtypeStruct(queries.shape, BF16)
    slim = jax.ShapeDtypeStruct(resp_keys.shape, BF16)
    return pl.pallas_call(
        prepare_kernel,
        out_shape=[wide, wide, slim, slim],
        in_specs=[SMEM, SMEM] + [ANY] * 5,
        out_specs=[VMEM] * 4,
        scratch_shapes=[pltpu.VMEM(table.shape, BF16), pltpu.SemaphoreType.DMA((5,))],
        compiler_params=SMALL,
        cost_estimate=pl.CostEstimate(
            flops=4 * queries.size, bytes_accessed=8 * queries.size, transcendentals=0
        ),
        name="prepare",
    )(pref_ids, resp_len, queries, out_grad, table, resp_keys, resp_values)


def chip_tile(r_ref, mate_ref):
    own = r_ref[...].astype(F32)[: RTILE // 2]
    mate = mate_ref[mate_ref.shape[0] - RTILE :, :].astype(F32)[: RTILE // 2]
    return jnp.concatenate([own, mate], axis=0).astype(BF16)


def pair_sum_kernel(tiles, direct_ref, got_ref, r_ref, mate_ref, *out_refs):
    at = 0
    for out, count in zip(out_refs, tiles):
        n = out.shape[0] - (RTILE if count else 0)
        total = direct_ref[at : at + n, :].astype(F32) + got_ref[at : at + n, :].astype(F32)
        out[:n, :] = total.astype(out.dtype)
        if count == 1:
            out[n:, :] = r_ref[...]
        if count == 2:
            out[n:, :] = chip_tile(r_ref, mate_ref)
        at += n


def pair_sum(direct, got, r_tile, mate, sizes, tiles):
    lanes = direct.shape[1]
    return pl.pallas_call(
        functools.partial(pair_sum_kernel, tiles),
        out_shape=[
            jax.ShapeDtypeStruct((n + RTILE if t else n, lanes), BF16 if t else F32)
            for n, t in zip(sizes, tiles)
        ],
        in_specs=[VMEM] * 4,
        out_specs=[VMEM] * len(sizes),
        compiler_params=SMALL,
        name="pair_sum",
    )(direct, got, r_tile, mate)


def middle_sum_kernel(two_ref, three_ref, four_ref, r_ref, got_ref, out_ref):
    rows = two_ref.shape[0]
    block = rows // 2
    total = two_ref[...] + three_ref[:rows, :].astype(F32)
    out_ref[:block, :] = (total[:block, :] + four_ref[:block, :].astype(F32)).astype(BF16)
    out_ref[block:rows, :] = total[block:, :].astype(BF16)
    out_ref[rows : rows + RTILE, :] = chip_tile(r_ref, got_ref)
    out_ref[rows + RTILE : rows + 2 * RTILE, :] = three_ref[rows:, :]
    out_ref[rows + 2 * RTILE :, :] = four_ref[block:, :]


def middle_sum(two, three, four, r_tile, got):
    return pl.pallas_call(
        middle_sum_kernel,
        out_shape=jax.ShapeDtypeStruct((two.shape[0] + 3 * RTILE, two.shape[1]), BF16),
        in_specs=[VMEM] * 5,
        out_specs=VMEM,
        compiler_params=SMALL,
        name="middle_sum",
    )(two, three, four, r_tile, got)


def chip_sum_kernel(near_ref, one_ref, two_ref, mine_ref, other_ref):
    rows = near_ref.shape[0]
    block = rows // 2
    total = near_ref[...].astype(F32) + one_ref[:rows, :].astype(F32) + two_ref[:rows, :].astype(F32)
    mine_ref[...] = total[:block, :]
    other_ref[:block, :] = total[block:, :].astype(BF16)
    split = block + one_ref.shape[0] - rows
    other_ref[block:split, :] = one_ref[rows:, :]
    other_ref[split:, :] = two_ref[rows:, :]


def chip_sum(near, one, two):
    rows, lanes = near.shape
    block = rows // 2
    sent = block + one.shape[0] + two.shape[0] - 2 * rows
    return pl.pallas_call(
        chip_sum_kernel,
        out_shape=[
            jax.ShapeDtypeStruct((block, lanes), F32),
            jax.ShapeDtypeStruct((sent, lanes), BF16),
        ],
        in_specs=[VMEM] * 3,
        out_specs=[VMEM] * 2,
        compiler_params=SMALL,
        name="chip_sum",
    )(near, one, two)


def last_sum_kernel(mine_ref, sent_ref, last_ref, r_ref, got_ref, dk_ref, dv_ref, pref_ref):
    block = mine_ref.shape[0]
    total = mine_ref[...] + last_ref[:block, :].astype(F32)
    dk_ref[...] = total[:, :HEAD_DIM].astype(BF16)
    dv_ref[...] = total[:, HEAD_DIM:].astype(BF16)
    n_pref, columns = pref_ref.shape
    lanes = mine_ref.shape[1]
    tiles = [chip_tile(r_ref, got_ref)]
    for ref in (sent_ref, last_ref):
        for at in range(block, ref.shape[0], RTILE):
            tiles.append(ref[at : at + RTILE, :])
    tiles = [t.astype(F32) for t in tiles]
    count = columns // lanes
    half = RTILE // 2
    tiles = [t[at : at + half, :] for t in tiles for at in (0, half)]
    hot = jnp.concatenate([t[count : count + 1, :n_pref] for t in tiles], axis=0)
    hot = hot.astype(BF16)
    for j in range(count):
        sums = jnp.concatenate([t[j : j + 1, :] for t in tiles], axis=0).astype(BF16)
        pref_ref[:, j * lanes : (j + 1) * lanes] = lax.dot_general(
            hot, sums, (((0,), (0,)), ((), ())), preferred_element_type=F32
        )


def last_sum(mine, sent, last, r_tile, got, n_pref, columns):
    block = mine.shape[0]
    return pl.pallas_call(
        last_sum_kernel,
        out_shape=[
            jax.ShapeDtypeStruct((block, HEAD_DIM), BF16),
            jax.ShapeDtypeStruct((block, HEAD_DIM), BF16),
            jax.ShapeDtypeStruct((n_pref, columns), F32),
        ],
        in_specs=[VMEM] * 5,
        out_specs=[VMEM] * 3,
        compiler_params=SMALL,
        name="last_sum",
    )(mine, sent, last, r_tile, got)


def in_hbm(array):
    return pltpu.with_memory_space_constraint(array, pltpu.HBM)


def shards(
    n_resp,
    queries,
    resp_keys,
    resp_values,
    prompt_keys,
    prompt_values,
    out_grad,
    pref_table,
    pref_ids,
    resp_len,
):
    pair, to_one, to_two, to_three, to_four = ring_moves(n_resp)

    def move(array, moves):
        return lax.ppermute(array, "resp", moves)

    block = prompt_keys.shape[0]
    arrays = (queries, out_grad, pref_table, resp_keys, resp_values)
    biased, masked, resp_keys, resp_values = prepare(
        pref_ids, resp_len, *[in_hbm(array) for array in arrays]
    )
    mate = [move(prompt_keys, pair), move(prompt_values, pair)]
    chip = assemble(pack(in_hbm(prompt_keys), in_hbm(prompt_values)), *mate)
    second = move(chip, to_two)
    first = move(chip, to_one)
    part0 = scores(biased, masked, [chip], (resp_keys, resp_values))
    second, part0 = lax.optimization_barrier((second, part0))
    third = move(second, to_three)
    fourth = move(second[:block], to_four)
    part1 = scores(biased, masked, [first, second])
    part2 = scores(biased, masked, [move(first, pair), move(second, pair)])
    third, fourth, part1, part2 = lax.optimization_barrier((third, fourth, part1, part2))
    part3 = scores(biased, masked, [third, fourth])
    part4 = scores(biased, masked, [move(third, pair), move(fourth, pair)])
    parts = [part0, part1, part2, part3, part4]
    lows, dps, stats, keys_t = zip(*parts)
    *ds, query_grad, scale, r_tile = query_side(
        pref_ids, lows, dps, stats, keys_t, queries.shape[0], queries.shape[1]
    )

    def keys_of(picks, near, *extra):
        some_ds, some_lows = [ds[i] for i in picks], [lows[i] for i in picks]
        return key_side(picks, scale, biased, masked, some_ds, some_lows, near, extra)

    direct_far, via_far = keys_of((3, 4), False, r_tile)
    got = move(via_far, pair)
    three, four = pair_sum(direct_far, got, r_tile, got, (2 * block, block), (2, 1))
    (via_close,) = keys_of((2,), False)
    (direct_close,) = keys_of((1,), False)
    one, two = pair_sum(
        direct_close, move(via_close, pair), r_tile, got, (2 * block, 2 * block), (2, 0)
    )
    near, resp_key_grad, resp_value_grad, query_grad = keys_of((0,), True, query_grad)
    four = move(four, to_four)
    three = move(three, to_three)
    one = move(one, to_one)
    two = move(middle_sum(two, three, four, r_tile, got), to_two)
    mine, sent = chip_sum(near, one, two)
    last = move(sent, pair)
    prompt_key_grad, prompt_value_grad, pref_grad = last_sum(
        mine, sent, last, r_tile, got, pref_table.shape[0], queries.shape[1]
    )
    return (
        query_grad,
        resp_key_grad,
        resp_value_grad,
        prompt_key_grad,
        prompt_value_grad,
        pref_grad,
    )


def solution(mesh):
    rows = P(("dp", "resp"), "tensor")
    in_specs = (rows,) * 6 + (P(None, "tensor"), P(("dp", "resp")), P(("dp", "resp")))
    out_specs = (rows,) * 5 + (P("dp", "tensor"),)
    return jax.shard_map(
        functools.partial(shards, mesh.shape["resp"]),
        mesh=mesh,
        in_specs=in_specs,
        out_specs=out_specs,
        check_vma=False,
    )
```

```python
import functools

import jax
import jax.numpy as jnp
from jax import lax
from jax.experimental import pallas as pl
from jax.experimental.pallas import tpu as pltpu
from jax.sharding import PartitionSpec as P

F32 = jnp.float32
BF16 = jnp.bfloat16
HEAD_DIM = 128
SCALING = HEAD_DIM**-0.5
LOG2E = 1.4426950408889634
HEADS_PER_STEP = 2
CHUNK = 256
RTILE = 16
NT = (((1,), (1,)), ((), ()))
NN = (((1,), (0,)), ((), ()))
VMEM = pl.BlockSpec(memory_space=pltpu.VMEM)
SMEM = pl.BlockSpec(memory_space=pltpu.SMEM)
ANY = pl.BlockSpec(memory_space=pltpu.HBM)
SMALL = pltpu.CompilerParams(vmem_limit_bytes=8 * 1024 * 1024)


def ring_moves(n_resp):
    chips = n_resp // 2
    places = [(chip, core) for chip in range(chips) for core in range(2)]

    def index(chip, core):
        return chip % chips * 2 + core

    def sign(chip, core, period):
        return 1 if (chip % period < period // 2) == (core == 0) else -1

    def reply_core(chip, neighbour):
        return 0 if sign(neighbour, 0, 4) == neighbour - chip else 1

    pair, one, two, three, four = [], [], [], [], []
    for z, c in places:
        me = index(z, c)
        pair.append((me, index(z, 1 - c)))
        one.append((me, index(z + sign(z, c, 2), c)))
        step = sign(z, c, 4)
        two.append((me, index(z + 2 * step, c)))
        three.append((me, index(z - step, reply_core(z, z - step))))
        four.append((me, index(z - 2 * step, c)))
    for moves in (pair, one, two, three, four):
        assert sorted(moves) == sorted((b, a) for a, b in moves)
    return pair, one, two, three, four


def scores_kernel(n_blocks, has_resp, q_ref, g_ref, *refs):
    block_refs = refs[:n_blocks]
    resp_refs = refs[n_blocks : n_blocks + 2 * has_resp]
    low_ref, dp_ref, stat_ref, keys_t_ref, *score_refs = refs[n_blocks + 2 * has_resp :]
    rows = q_ref.shape[0]
    factor = SCALING * LOG2E
    pieces = []
    at = 0
    for ref in block_refs:
        n = ref.shape[0]
        pieces.append((at, n, ref.at[:, :HEAD_DIM], ref.at[:, HEAD_DIM:], False))
        at += n
    if has_resp:
        pieces.append((at, rows, resp_refs[0], resp_refs[1], True))
    for at, n, key_ref, _, _ in pieces:
        keys_t_ref[:, at : at + n] = key_ref[...].T

    def score(head, piece, top):
        at, n, key_ref, _, is_resp = piece
        q = q_ref[:, head * HEAD_DIM : (head + 1) * HEAD_DIM]
        s = lax.dot_general(key_ref[...], q, NT, preferred_element_type=F32)
        if is_resp:
            key_pos = lax.broadcasted_iota(jnp.int32, (n, rows), 0)
            query_pos = lax.broadcasted_iota(jnp.int32, (n, rows), 1)
            s = jnp.where(key_pos <= query_pos, s, -1e30)
        score_refs[head % 3][at : at + n, :] = s
        return jnp.maximum(top, jnp.max(s.reshape(n // 8, 8, rows), axis=0))

    lowest = jnp.full((8, rows), -1e30, F32)
    heads = q_ref.shape[1] // HEAD_DIM
    tops = [lowest] * heads
    for head in range(2):
        for piece in pieces:
            tops[head] = score(head, piece, tops[head])
    for head in range(heads):
        cols = slice(head * rows, (head + 1) * rows)
        g = g_ref[:, head * HEAD_DIM : (head + 1) * HEAD_DIM]
        row_max = jnp.max(tops[head], axis=0, keepdims=True) * factor
        total = jnp.zeros((8, rows), F32)
        dot = jnp.zeros((8, rows), F32)
        for piece in pieces:
            at, n, _, value_ref, _ = piece
            p = jnp.exp2(score_refs[head % 3][at : at + n, :] * factor - row_max)
            dp = lax.dot_general(value_ref[...], g, NT, preferred_element_type=F32)
            total = total + jnp.sum(p.reshape(n // 8, 8, rows), axis=0)
            dot = dot + jnp.sum((p * dp).reshape(n // 8, 8, rows), axis=0)
            low_ref[at : at + n, cols] = p.astype(BF16)
            dp_ref[at : at + n, cols] = dp
            if head + 2 < heads:
                tops[head + 2] = score(head + 2, piece, tops[head + 2])
        stat_ref[0:1, cols] = row_max
        stat_ref[1:2, cols] = jnp.sum(total, axis=0, keepdims=True)
        stat_ref[2:3, cols] = jnp.sum(dot, axis=0, keepdims=True)


def scores(biased, masked, blocks, resp=()):
    rows, columns = biased.shape
    n = sum(b.shape[0] for b in blocks) + (rows if resp else 0)
    queries = rows * columns // HEAD_DIM
    shape = jax.ShapeDtypeStruct
    return pl.pallas_call(
        functools.partial(scores_kernel, len(blocks), bool(resp)),
        out_shape=[
            shape((n, queries), BF16),
            shape((n, queries), F32),
            shape((8, queries), F32),
            shape((HEAD_DIM, n), BF16),
        ],
        in_specs=[VMEM] * (2 + len(blocks) + len(resp)),
        out_specs=[VMEM] * 4,
        scratch_shapes=[pltpu.VMEM((n, rows), F32)] * 3,
        compiler_params=SMALL,
        cost_estimate=pl.CostEstimate(
            flops=4 * n * queries * HEAD_DIM, bytes_accessed=0, transcendentals=n * queries
        ),
        name="scores",
    )(biased, masked, *blocks, *resp)


def query_kernel(count, id_ref, *refs):
    low_refs = refs[:count]
    dp_refs = refs[count : 2 * count]
    stat_refs = refs[2 * count : 3 * count]
    key_refs = refs[3 * count : 4 * count]
    ds_refs = refs[4 * count : 5 * count]
    dq_ref, scale_ref, r_ref, sum_scr, delta_scr = refs[5 * count :]
    rows, columns = dq_ref.shape
    width = HEADS_PER_STEP * rows
    top = stat_refs[0][0:1, :]
    for ref in stat_refs[1:]:
        top = jnp.maximum(top, ref[0:1, :])
    total = dot = 0.0
    for i, ref in enumerate(stat_refs):
        shift = jnp.exp2(ref[0:1, :] - top)
        scale_ref[i : i + 1, :] = shift
        total = total + ref[1:2, :] * shift
        dot = dot + ref[2:3, :] * shift
    inverse = 1.0 / total
    delta_scr[...] = dot * inverse
    for i in range(count):
        scale_ref[i : i + 1, :] = scale_ref[i : i + 1, :] * inverse
    for group in range(columns // (HEADS_PER_STEP * HEAD_DIM)):
        cols = slice(group * width, (group + 1) * width)
        delta = delta_scr[:, cols]
        dq = jnp.zeros((HEAD_DIM, width), F32)
        for i in range(count):
            ds = low_refs[i][:, cols] * (dp_refs[i][:, cols] - delta).astype(BF16)
            ds_refs[i][:, cols] = ds
            part = lax.dot_general(key_refs[i][...], ds, NN, preferred_element_type=F32)
            dq = dq + part * scale_ref[i : i + 1, cols]
        dq = dq.T * SCALING
        for i in range(HEADS_PER_STEP):
            at = (group * HEADS_PER_STEP + i) * HEAD_DIM
            part = dq[i * rows : (i + 1) * rows]
            dq_ref[:, at : at + HEAD_DIM] = part.astype(BF16)
            sum_scr[:, at : at + HEAD_DIM] = jnp.sum(part, axis=0, keepdims=True)
    lanes = 2 * HEAD_DIM
    pieces = [sum_scr[:, j * lanes : (j + 1) * lanes] for j in range(columns // lanes)]
    hot = (lax.broadcasted_iota(jnp.int32, (1, lanes), 1) == id_ref[0]).astype(F32)
    blank = jnp.zeros((RTILE - columns // lanes - 1, lanes), F32)
    r_ref[...] = jnp.concatenate(pieces + [hot, blank], axis=0).astype(BF16)


def query_side(pref_ids, lows, dps, stats, keys_t, rows, columns):
    count = len(lows)
    queries = lows[0].shape[1]
    shape = jax.ShapeDtypeStruct
    keys = sum(low.shape[0] for low in lows)
    return pl.pallas_call(
        functools.partial(query_kernel, count),
        out_shape=[shape(low.shape, BF16) for low in lows]
        + [
            shape((rows, columns), BF16),
            shape((8, queries), F32),
            shape((RTILE, 2 * HEAD_DIM), BF16),
        ],
        in_specs=[SMEM] + [VMEM] * (4 * count),
        out_specs=[VMEM] * (count + 3),
        scratch_shapes=[pltpu.VMEM((1, columns), F32), pltpu.VMEM((1, queries), F32)],
        compiler_params=SMALL,
        cost_estimate=pl.CostEstimate(
            flops=2 * keys * queries * HEAD_DIM, bytes_accessed=0, transcendentals=0
        ),
        name="query_side",
    )(pref_ids, *lows, *dps, *stats, *keys_t)


def key_kernel(picks, extra, scale_ref, q_ref, g_ref, *refs):
    count = len(picks)
    ds_refs = refs[:count]
    low_refs = refs[count : 2 * count]
    extra_refs = refs[2 * count : 2 * count + extra]
    *out_refs, q_scr, g_scr, sem = refs[2 * count + extra :]
    is_near = len(out_refs) > 2
    if is_near:
        flush = pltpu.make_async_copy(extra_refs[0], out_refs[3], sem)
        flush.start()
    rows = q_ref.shape[0]
    results = []
    for i, pick in enumerate(picks):
        for head in range(q_ref.shape[1] // HEAD_DIM):
            at = slice(head * rows, (head + 1) * rows)
            cols = slice(head * HEAD_DIM, (head + 1) * HEAD_DIM)
            scale = jnp.broadcast_to(scale_ref[pick : pick + 1, at], (HEAD_DIM, rows)).T
            q_scr[i, at, :] = (q_ref[:, cols].astype(F32) * scale).astype(BF16)
            g_scr[i, at, :] = (g_ref[:, cols].astype(F32) * scale).astype(BF16)
        dk = lax.dot_general(ds_refs[i][...], q_scr[i], NN, preferred_element_type=F32) * SCALING
        dv = lax.dot_general(low_refs[i][...], g_scr[i], NN, preferred_element_type=F32)
        results.append((dk.astype(BF16), dv.astype(BF16)))
    if not is_near:
        for ref, (dk, dv) in zip(out_refs, results):
            n = dk.shape[0]
            ref[:n, :HEAD_DIM] = dk
            ref[:n, HEAD_DIM:] = dv
        if extra:
            out_refs[-1][n:, :] = extra_refs[0][...]
    else:
        near_ref, drk_ref, drv_ref, _ = out_refs
        n = near_ref.shape[0]
        dk, dv = results[0]
        near_ref[:, :HEAD_DIM] = dk[:n, :]
        near_ref[:, HEAD_DIM:] = dv[:n, :]
        drk_ref[...] = dk[n:, :]
        drv_ref[...] = dv[n:, :]
        flush.wait()


def key_side(picks, scale, biased, masked, ds, lows, near, extra):
    rows, columns = biased.shape
    queries = rows * columns // HEAD_DIM
    lanes = 2 * HEAD_DIM
    if not near:
        counts = [d.shape[0] for d in ds]
        counts[-1] += RTILE * len(extra)
        shapes = [(n, lanes) for n in counts]
    else:
        shapes = [(ds[0].shape[0] - rows, lanes), (rows, HEAD_DIM), (rows, HEAD_DIM)]
        shapes.append((rows, columns))
    keys = sum(d.shape[0] for d in ds)
    return pl.pallas_call(
        functools.partial(key_kernel, picks, len(extra)),
        out_shape=[jax.ShapeDtypeStruct(s, BF16) for s in shapes],
        in_specs=[VMEM] * (3 + 2 * len(picks) + len(extra)),
        out_specs=[VMEM] * 3 + [ANY] if near else [VMEM] * len(shapes),
        scratch_shapes=[pltpu.VMEM((len(picks), queries, HEAD_DIM), BF16)] * 2
        + [pltpu.SemaphoreType.DMA],
        compiler_params=SMALL,
        cost_estimate=pl.CostEstimate(
            flops=4 * keys * queries * HEAD_DIM, bytes_accessed=0, transcendentals=0
        ),
        name="key_side",
    )(scale, biased, masked, *ds, *lows, *extra)


def pack_kernel(k_ref, v_ref, own_ref, sems):
    copies = [
        pltpu.make_async_copy(k_ref, own_ref.at[:, :HEAD_DIM], sems.at[0]),
        pltpu.make_async_copy(v_ref, own_ref.at[:, HEAD_DIM:], sems.at[1]),
    ]
    for copy in copies:
        copy.start()
    for copy in copies:
        copy.wait()


def pack(keys, values):
    return pl.pallas_call(
        pack_kernel,
        out_shape=jax.ShapeDtypeStruct((keys.shape[0], 2 * HEAD_DIM), BF16),
        in_specs=[ANY, ANY],
        out_specs=VMEM,
        scratch_shapes=[pltpu.SemaphoreType.DMA((2,))],
        compiler_params=SMALL,
        name="pack",
    )(keys, values)


def assemble_kernel(own_ref, k_ref, v_ref, chip_ref):
    n = own_ref.shape[0]
    chip_ref[:n, :] = own_ref[...]
    chip_ref[n:, :HEAD_DIM] = k_ref[...]
    chip_ref[n:, HEAD_DIM:] = v_ref[...]


def assemble(own, keys, values):
    return pl.pallas_call(
        assemble_kernel,
        out_shape=jax.ShapeDtypeStruct((2 * own.shape[0], own.shape[1]), BF16),
        in_specs=[VMEM] * 3,
        out_specs=VMEM,
        compiler_params=SMALL,
        name="assemble",
    )(own, keys, values)


def prepare_kernel(
    id_ref,
    len_ref,
    q_hbm,
    g_hbm,
    table_hbm,
    rk_hbm,
    rv_hbm,
    biased_ref,
    masked_ref,
    rk_ref,
    rv_ref,
    table_ref,
    sems,
):
    arrays = [
        (table_hbm, table_ref),
        (q_hbm, biased_ref),
        (g_hbm, masked_ref),
        (rk_hbm, rk_ref),
        (rv_hbm, rv_ref),
    ]
    copies = [pltpu.make_async_copy(a, b, sems.at[i]) for i, (a, b) in enumerate(arrays)]
    for copy in copies:
        copy.start()
    copies[0].wait()
    chosen = lax.broadcasted_iota(jnp.int32, table_ref.shape, 0) == id_ref[0]
    pref = jnp.sum(jnp.where(chosen, table_ref[...].astype(F32), 0.0), axis=0, keepdims=True)
    copies[1].wait()
    biased_ref[...] = (biased_ref[...].astype(F32) + pref).astype(BF16)
    copies[2].wait()
    live = lax.broadcasted_iota(jnp.int32, masked_ref.shape, 0) < len_ref[0]
    masked_ref[...] = jnp.where(live, masked_ref[...], jnp.zeros((), BF16))
    copies[3].wait()
    copies[4].wait()


def prepare(pref_ids, resp_len, queries, out_grad, table, resp_keys, resp_values):
    wide = jax.ShapeDtypeStruct(queries.shape, BF16)
    slim = jax.ShapeDtypeStruct(resp_keys.shape, BF16)
    return pl.pallas_call(
        prepare_kernel,
        out_shape=[wide, wide, slim, slim],
        in_specs=[SMEM, SMEM] + [ANY] * 5,
        out_specs=[VMEM] * 4,
        scratch_shapes=[pltpu.VMEM(table.shape, BF16), pltpu.SemaphoreType.DMA((5,))],
        compiler_params=SMALL,
        cost_estimate=pl.CostEstimate(
            flops=4 * queries.size, bytes_accessed=8 * queries.size, transcendentals=0
        ),
        name="prepare",
    )(pref_ids, resp_len, queries, out_grad, table, resp_keys, resp_values)


def chip_tile(r_ref, mate_ref):
    own = r_ref[...].astype(F32)[: RTILE // 2]
    mate = mate_ref[mate_ref.shape[0] - RTILE :, :].astype(F32)[: RTILE // 2]
    return jnp.concatenate([own, mate], axis=0).astype(BF16)


def pair_sum_kernel(tiles, direct_ref, got_ref, r_ref, mate_ref, *out_refs):
    at = 0
    for out, count in zip(out_refs, tiles):
        n = out.shape[0] - (RTILE if count else 0)
        total = direct_ref[at : at + n, :].astype(F32) + got_ref[at : at + n, :].astype(F32)
        out[:n, :] = total.astype(out.dtype)
        if count == 1:
            out[n:, :] = r_ref[...]
        if count == 2:
            out[n:, :] = chip_tile(r_ref, mate_ref)
        at += n


def pair_sum(direct, got, r_tile, mate, sizes, tiles):
    lanes = direct.shape[1]
    return pl.pallas_call(
        functools.partial(pair_sum_kernel, tiles),
        out_shape=[
            jax.ShapeDtypeStruct((n + RTILE if t else n, lanes), BF16 if t else F32)
            for n, t in zip(sizes, tiles)
        ],
        in_specs=[VMEM] * 4,
        out_specs=[VMEM] * len(sizes),
        compiler_params=SMALL,
        name="pair_sum",
    )(direct, got, r_tile, mate)


def middle_sum_kernel(two_ref, three_ref, four_ref, r_ref, got_ref, out_ref):
    rows = two_ref.shape[0]
    block = rows // 2
    total = two_ref[...] + three_ref[:rows, :].astype(F32)
    out_ref[:block, :] = (total[:block, :] + four_ref[:block, :].astype(F32)).astype(BF16)
    out_ref[block:rows, :] = total[block:, :].astype(BF16)
    out_ref[rows : rows + RTILE, :] = chip_tile(r_ref, got_ref)
    out_ref[rows + RTILE : rows + 2 * RTILE, :] = three_ref[rows:, :]
    out_ref[rows + 2 * RTILE :, :] = four_ref[block:, :]


def middle_sum(two, three, four, r_tile, got):
    return pl.pallas_call(
        middle_sum_kernel,
        out_shape=jax.ShapeDtypeStruct((two.shape[0] + 3 * RTILE, two.shape[1]), BF16),
        in_specs=[VMEM] * 5,
        out_specs=VMEM,
        compiler_params=SMALL,
        name="middle_sum",
    )(two, three, four, r_tile, got)


def chip_sum_kernel(near_ref, one_ref, two_ref, mine_ref, other_ref):
    rows = near_ref.shape[0]
    block = rows // 2
    total = near_ref[...].astype(F32) + one_ref[:rows, :].astype(F32) + two_ref[:rows, :].astype(F32)
    mine_ref[...] = total[:block, :]
    other_ref[:block, :] = total[block:, :].astype(BF16)
    split = block + one_ref.shape[0] - rows
    other_ref[block:split, :] = one_ref[rows:, :]
    other_ref[split:, :] = two_ref[rows:, :]


def chip_sum(near, one, two):
    rows, lanes = near.shape
    block = rows // 2
    sent = block + one.shape[0] + two.shape[0] - 2 * rows
    return pl.pallas_call(
        chip_sum_kernel,
        out_shape=[
            jax.ShapeDtypeStruct((block, lanes), F32),
            jax.ShapeDtypeStruct((sent, lanes), BF16),
        ],
        in_specs=[VMEM] * 3,
        out_specs=[VMEM] * 2,
        compiler_params=SMALL,
        name="chip_sum",
    )(near, one, two)


def last_sum_kernel(mine_ref, sent_ref, last_ref, r_ref, got_ref, dk_ref, dv_ref, pref_ref):
    block = mine_ref.shape[0]
    total = mine_ref[...] + last_ref[:block, :].astype(F32)
    dk_ref[...] = total[:, :HEAD_DIM].astype(BF16)
    dv_ref[...] = total[:, HEAD_DIM:].astype(BF16)
    n_pref, columns = pref_ref.shape
    lanes = mine_ref.shape[1]
    tiles = [chip_tile(r_ref, got_ref)]
    for ref in (sent_ref, last_ref):
        for at in range(block, ref.shape[0], RTILE):
            tiles.append(ref[at : at + RTILE, :])
    tiles = [t.astype(F32) for t in tiles]
    count = columns // lanes
    half = RTILE // 2
    tiles = [t[at : at + half, :] for t in tiles for at in (0, half)]
    hot = jnp.concatenate([t[count : count + 1, :n_pref] for t in tiles], axis=0)
    hot = hot.astype(BF16)
    for j in range(count):
        sums = jnp.concatenate([t[j : j + 1, :] for t in tiles], axis=0).astype(BF16)
        pref_ref[:, j * lanes : (j + 1) * lanes] = lax.dot_general(
            hot, sums, (((0,), (0,)), ((), ())), preferred_element_type=F32
        )


def last_sum(mine, sent, last, r_tile, got, n_pref, columns):
    block = mine.shape[0]
    return pl.pallas_call(
        last_sum_kernel,
        out_shape=[
            jax.ShapeDtypeStruct((block, HEAD_DIM), BF16),
            jax.ShapeDtypeStruct((block, HEAD_DIM), BF16),
            jax.ShapeDtypeStruct((n_pref, columns), F32),
        ],
        in_specs=[VMEM] * 5,
        out_specs=[VMEM] * 3,
        compiler_params=SMALL,
        name="last_sum",
    )(mine, sent, last, r_tile, got)


def in_hbm(array):
    return pltpu.with_memory_space_constraint(array, pltpu.HBM)


def shards(
    n_resp,
    queries,
    resp_keys,
    resp_values,
    prompt_keys,
    prompt_values,
    out_grad,
    pref_table,
    pref_ids,
    resp_len,
):
    pair, to_one, to_two, to_three, to_four = ring_moves(n_resp)

    def move(array, moves):
        return lax.ppermute(array, "resp", moves)

    block = prompt_keys.shape[0]
    arrays = (queries, out_grad, pref_table, resp_keys, resp_values)
    biased, masked, resp_keys, resp_values = prepare(
        pref_ids, resp_len, *[in_hbm(array) for array in arrays]
    )
    mate = [move(prompt_keys, pair), move(prompt_values, pair)]
    chip = assemble(pack(in_hbm(prompt_keys), in_hbm(prompt_values)), *mate)
    second = move(chip, to_two)
    first = move(chip, to_one)
    part0 = scores(biased, masked, [chip], (resp_keys, resp_values))
    second, part0 = lax.optimization_barrier((second, part0))
    third = move(second, to_three)
    fourth = move(second[:block], to_four)
    part1 = scores(biased, masked, [first, second])
    part2 = scores(biased, masked, [move(first, pair), move(second, pair)])
    third, fourth, part1, part2 = lax.optimization_barrier((third, fourth, part1, part2))
    part3 = scores(biased, masked, [third, fourth])
    part4 = scores(biased, masked, [move(third, pair), move(fourth, pair)])
    parts = [part0, part1, part2, part3, part4]
    lows, dps, stats, keys_t = zip(*parts)
    *ds, query_grad, scale, r_tile = query_side(
        pref_ids, lows, dps, stats, keys_t, queries.shape[0], queries.shape[1]
    )

    def keys_of(picks, near, *extra):
        some_ds, some_lows = [ds[i] for i in picks], [lows[i] for i in picks]
        return key_side(picks, scale, biased, masked, some_ds, some_lows, near, extra)

    direct_far, via_far = keys_of((3, 4), False, r_tile)
    got = move(via_far, pair)
    three, four = pair_sum(direct_far, got, r_tile, got, (2 * block, block), (2, 1))
    (via_close,) = keys_of((2,), False)
    (direct_close,) = keys_of((1,), False)
    one, two = pair_sum(
        direct_close, move(via_close, pair), r_tile, got, (2 * block, 2 * block), (2, 0)
    )
    four = move(four, to_four)
    three = move(three, to_three)
    one = move(one, to_one)
    two = move(middle_sum(two, three, four, r_tile, got), to_two)
    scale, one = lax.optimization_barrier((scale, one))
    near, resp_key_grad, resp_value_grad, query_grad = keys_of((0,), True, query_grad)
    mine, sent = chip_sum(near, one, two)
    last = move(sent, pair)
    prompt_key_grad, prompt_value_grad, pref_grad = last_sum(
        mine, sent, last, r_tile, got, pref_table.shape[0], queries.shape[1]
    )
    return (
        query_grad,
        resp_key_grad,
        resp_value_grad,
        prompt_key_grad,
        prompt_value_grad,
        pref_grad,
    )


def solution(mesh):
    rows = P(("dp", "resp"), "tensor")
    in_specs = (rows,) * 6 + (P(None, "tensor"), P(("dp", "resp")), P(("dp", "resp")))
    out_specs = (rows,) * 5 + (P("dp", "tensor"),)
    return jax.shard_map(
        functools.partial(shards, mesh.shape["resp"]),
        mesh=mesh,
        in_specs=in_specs,
        out_specs=out_specs,
        check_vma=False,
    )
```

```python
import functools

import jax
import jax.numpy as jnp
from jax import lax
from jax.experimental import pallas as pl
from jax.experimental.pallas import tpu as pltpu
from jax.sharding import PartitionSpec as P

F32 = jnp.float32
BF16 = jnp.bfloat16
HEAD_DIM = 128
SCALING = HEAD_DIM**-0.5
LOG2E = 1.4426950408889634
HEADS_PER_STEP = 4
CHUNK = 256
RTILE = 16
NT = (((1,), (1,)), ((), ()))
NN = (((1,), (0,)), ((), ()))
VMEM = pl.BlockSpec(memory_space=pltpu.VMEM)
SMEM = pl.BlockSpec(memory_space=pltpu.SMEM)
ANY = pl.BlockSpec(memory_space=pltpu.HBM)
SMALL = pltpu.CompilerParams(vmem_limit_bytes=8 * 1024 * 1024)


def ring_moves(n_resp):
    chips = n_resp // 2
    places = [(chip, core) for chip in range(chips) for core in range(2)]

    def index(chip, core):
        return chip % chips * 2 + core

    def sign(chip, core, period):
        return 1 if (chip % period < period // 2) == (core == 0) else -1

    def reply_core(chip, neighbour):
        return 0 if sign(neighbour, 0, 4) == neighbour - chip else 1

    pair, one, two, three, four = [], [], [], [], []
    for z, c in places:
        me = index(z, c)
        pair.append((me, index(z, 1 - c)))
        one.append((me, index(z + sign(z, c, 2), c)))
        step = sign(z, c, 4)
        two.append((me, index(z + 2 * step, c)))
        three.append((me, index(z - step, reply_core(z, z - step))))
        four.append((me, index(z - 2 * step, c)))
    for moves in (pair, one, two, three, four):
        assert sorted(moves) == sorted((b, a) for a, b in moves)
    return pair, one, two, three, four


def scores_kernel(n_blocks, has_resp, q_ref, g_ref, *refs):
    block_refs = refs[:n_blocks]
    resp_refs = refs[n_blocks : n_blocks + 2 * has_resp]
    low_ref, dp_ref, stat_ref, keys_t_ref, *score_refs = refs[n_blocks + 2 * has_resp :]
    rows = q_ref.shape[0]
    factor = SCALING * LOG2E
    pieces = []
    at = 0
    for ref in block_refs:
        n = ref.shape[0]
        pieces.append((at, n, ref.at[:, :HEAD_DIM], ref.at[:, HEAD_DIM:], False))
        at += n
    if has_resp:
        pieces.append((at, rows, resp_refs[0], resp_refs[1], True))
    for at, n, key_ref, _, _ in pieces:
        keys_t_ref[:, at : at + n] = key_ref[...].T

    def score(head, piece, top):
        at, n, key_ref, _, is_resp = piece
        q = q_ref[:, head * HEAD_DIM : (head + 1) * HEAD_DIM]
        s = lax.dot_general(key_ref[...], q, NT, preferred_element_type=F32)
        if is_resp:
            key_pos = lax.broadcasted_iota(jnp.int32, (n, rows), 0)
            query_pos = lax.broadcasted_iota(jnp.int32, (n, rows), 1)
            s = jnp.where(key_pos <= query_pos, s, -1e30)
        score_refs[head % 3][at : at + n, :] = s
        return jnp.maximum(top, jnp.max(s.reshape(n // 8, 8, rows), axis=0))

    lowest = jnp.full((8, rows), -1e30, F32)
    heads = q_ref.shape[1] // HEAD_DIM
    tops = [lowest] * heads
    for head in range(2):
        for piece in pieces:
            tops[head] = score(head, piece, tops[head])
    for head in range(heads):
        cols = slice(head * rows, (head + 1) * rows)
        g = g_ref[:, head * HEAD_DIM : (head + 1) * HEAD_DIM]
        row_max = jnp.max(tops[head], axis=0, keepdims=True) * factor
        total = jnp.zeros((8, rows), F32)
        dot = jnp.zeros((8, rows), F32)
        for piece in pieces:
            at, n, _, value_ref, _ = piece
            p = jnp.exp2(score_refs[head % 3][at : at + n, :] * factor - row_max)
            dp = lax.dot_general(value_ref[...], g, NT, preferred_element_type=F32)
            total = total + jnp.sum(p.reshape(n // 8, 8, rows), axis=0)
            dot = dot + jnp.sum((p * dp).reshape(n // 8, 8, rows), axis=0)
            low_ref[at : at + n, cols] = p.astype(BF16)
            dp_ref[at : at + n, cols] = dp
            if head + 2 < heads:
                tops[head + 2] = score(head + 2, piece, tops[head + 2])
        stat_ref[0:1, cols] = row_max
        stat_ref[1:2, cols] = jnp.sum(total, axis=0, keepdims=True)
        stat_ref[2:3, cols] = jnp.sum(dot, axis=0, keepdims=True)


def scores(biased, masked, blocks, resp=()):
    rows, columns = biased.shape
    n = sum(b.shape[0] for b in blocks) + (rows if resp else 0)
    queries = rows * columns // HEAD_DIM
    shape = jax.ShapeDtypeStruct
    return pl.pallas_call(
        functools.partial(scores_kernel, len(blocks), bool(resp)),
        out_shape=[
            shape((n, queries), BF16),
            shape((n, queries), F32),
            shape((8, queries), F32),
            shape((HEAD_DIM, n), BF16),
        ],
        in_specs=[VMEM] * (2 + len(blocks) + len(resp)),
        out_specs=[VMEM] * 4,
        scratch_shapes=[pltpu.VMEM((n, rows), F32)] * 3,
        compiler_params=SMALL,
        cost_estimate=pl.CostEstimate(
            flops=4 * n * queries * HEAD_DIM, bytes_accessed=0, transcendentals=n * queries
        ),
        name="scores",
    )(biased, masked, *blocks, *resp)


def query_kernel(count, id_ref, *refs):
    low_refs = refs[:count]
    dp_refs = refs[count : 2 * count]
    stat_refs = refs[2 * count : 3 * count]
    key_refs = refs[3 * count : 4 * count]
    ds_refs = refs[4 * count : 5 * count]
    dq_ref, scale_ref, r_ref, sum_scr, delta_scr = refs[5 * count :]
    rows, columns = dq_ref.shape
    width = HEADS_PER_STEP * rows
    top = stat_refs[0][0:1, :]
    for ref in stat_refs[1:]:
        top = jnp.maximum(top, ref[0:1, :])
    total = dot = 0.0
    for i, ref in enumerate(stat_refs):
        shift = jnp.exp2(ref[0:1, :] - top)
        scale_ref[i : i + 1, :] = shift
        total = total + ref[1:2, :] * shift
        dot = dot + ref[2:3, :] * shift
    inverse = 1.0 / total
    delta_scr[...] = dot * inverse
    for i in range(count):
        scale_ref[i : i + 1, :] = scale_ref[i : i + 1, :] * inverse
    for group in range(columns // (HEADS_PER_STEP * HEAD_DIM)):
        cols = slice(group * width, (group + 1) * width)
        delta = delta_scr[:, cols]
        dq = jnp.zeros((HEAD_DIM, width), F32)
        for i in range(count):
            ds = low_refs[i][:, cols] * (dp_refs[i][:, cols] - delta).astype(BF16)
            ds_refs[i][:, cols] = ds
            part = lax.dot_general(key_refs[i][...], ds, NN, preferred_element_type=F32)
            dq = dq + part * scale_ref[i : i + 1, cols]
        dq = dq.T * SCALING
        for i in range(HEADS_PER_STEP):
            at = (group * HEADS_PER_STEP + i) * HEAD_DIM
            part = dq[i * rows : (i + 1) * rows]
            dq_ref[:, at : at + HEAD_DIM] = part.astype(BF16)
            sum_scr[:, at : at + HEAD_DIM] = jnp.sum(part, axis=0, keepdims=True)
    lanes = 2 * HEAD_DIM
    pieces = [sum_scr[:, j * lanes : (j + 1) * lanes] for j in range(columns // lanes)]
    hot = (lax.broadcasted_iota(jnp.int32, (1, lanes), 1) == id_ref[0]).astype(F32)
    blank = jnp.zeros((RTILE - columns // lanes - 1, lanes), F32)
    r_ref[...] = jnp.concatenate(pieces + [hot, blank], axis=0).astype(BF16)


def query_side(pref_ids, lows, dps, stats, keys_t, rows, columns):
    count = len(lows)
    queries = lows[0].shape[1]
    shape = jax.ShapeDtypeStruct
    keys = sum(low.shape[0] for low in lows)
    return pl.pallas_call(
        functools.partial(query_kernel, count),
        out_shape=[shape(low.shape, BF16) for low in lows]
        + [
            shape((rows, columns), BF16),
            shape((8, queries), F32),
            shape((RTILE, 2 * HEAD_DIM), BF16),
        ],
        in_specs=[SMEM] + [VMEM] * (4 * count),
        out_specs=[VMEM] * (count + 3),
        scratch_shapes=[pltpu.VMEM((1, columns), F32), pltpu.VMEM((1, queries), F32)],
        compiler_params=SMALL,
        cost_estimate=pl.CostEstimate(
            flops=2 * keys * queries * HEAD_DIM, bytes_accessed=0, transcendentals=0
        ),
        name="query_side",
    )(pref_ids, *lows, *dps, *stats, *keys_t)


def key_kernel(picks, extra, scale_ref, q_ref, g_ref, *refs):
    count = len(picks)
    ds_refs = refs[:count]
    low_refs = refs[count : 2 * count]
    extra_refs = refs[2 * count : 2 * count + extra]
    *out_refs, q_scr, g_scr = refs[2 * count + extra :]
    is_near = len(out_refs) > 2
    rows = q_ref.shape[0]
    results = []
    for i, pick in enumerate(picks):
        for head in range(q_ref.shape[1] // HEAD_DIM):
            at = slice(head * rows, (head + 1) * rows)
            cols = slice(head * HEAD_DIM, (head + 1) * HEAD_DIM)
            scale = jnp.broadcast_to(scale_ref[pick : pick + 1, at], (HEAD_DIM, rows)).T
            q_scr[i, at, :] = (q_ref[:, cols].astype(F32) * scale).astype(BF16)
            g_scr[i, at, :] = (g_ref[:, cols].astype(F32) * scale).astype(BF16)
        dk = lax.dot_general(ds_refs[i][...], q_scr[i], NN, preferred_element_type=F32) * SCALING
        dv = lax.dot_general(low_refs[i][...], g_scr[i], NN, preferred_element_type=F32)
        results.append((dk.astype(BF16), dv.astype(BF16)))
    if not is_near:
        for ref, (dk, dv) in zip(out_refs, results):
            n = dk.shape[0]
            ref[:n, :HEAD_DIM] = dk
            ref[:n, HEAD_DIM:] = dv
        if extra:
            out_refs[-1][n:, :] = extra_refs[0][...]
    else:
        near_ref, drk_ref, drv_ref = out_refs
        n = near_ref.shape[0]
        dk, dv = results[0]
        near_ref[:, :HEAD_DIM] = dk[:n, :]
        near_ref[:, HEAD_DIM:] = dv[:n, :]
        drk_ref[...] = dk[n:, :]
        drv_ref[...] = dv[n:, :]


def key_side(picks, scale, biased, masked, ds, lows, near, extra):
    rows, columns = biased.shape
    queries = rows * columns // HEAD_DIM
    lanes = 2 * HEAD_DIM
    if not near:
        counts = [d.shape[0] for d in ds]
        counts[-1] += RTILE * len(extra)
        shapes = [(n, lanes) for n in counts]
    else:
        shapes = [(ds[0].shape[0] - rows, lanes), (rows, HEAD_DIM), (rows, HEAD_DIM)]
    keys = sum(d.shape[0] for d in ds)
    return pl.pallas_call(
        functools.partial(key_kernel, picks, len(extra)),
        out_shape=[jax.ShapeDtypeStruct(s, BF16) for s in shapes],
        in_specs=[VMEM] * (3 + 2 * len(picks) + len(extra)),
        out_specs=[VMEM] * len(shapes),
        scratch_shapes=[pltpu.VMEM((len(picks), queries, HEAD_DIM), BF16)] * 2,
        compiler_params=SMALL,
        cost_estimate=pl.CostEstimate(
            flops=4 * keys * queries * HEAD_DIM, bytes_accessed=0, transcendentals=0
        ),
        name="key_side",
    )(scale, biased, masked, *ds, *lows, *extra)


def pack_kernel(k_ref, v_ref, own_ref, sems):
    copies = [
        pltpu.make_async_copy(k_ref, own_ref.at[:, :HEAD_DIM], sems.at[0]),
        pltpu.make_async_copy(v_ref, own_ref.at[:, HEAD_DIM:], sems.at[1]),
    ]
    for copy in copies:
        copy.start()
    for copy in copies:
        copy.wait()


def pack(keys, values):
    return pl.pallas_call(
        pack_kernel,
        out_shape=jax.ShapeDtypeStruct((keys.shape[0], 2 * HEAD_DIM), BF16),
        in_specs=[ANY, ANY],
        out_specs=VMEM,
        scratch_shapes=[pltpu.SemaphoreType.DMA((2,))],
        compiler_params=SMALL,
        name="pack",
    )(keys, values)


def assemble_kernel(own_ref, k_ref, v_ref, chip_ref):
    n = own_ref.shape[0]
    chip_ref[:n, :] = own_ref[...]
    chip_ref[n:, :HEAD_DIM] = k_ref[...]
    chip_ref[n:, HEAD_DIM:] = v_ref[...]


def assemble(own, keys, values):
    return pl.pallas_call(
        assemble_kernel,
        out_shape=jax.ShapeDtypeStruct((2 * own.shape[0], own.shape[1]), BF16),
        in_specs=[VMEM] * 3,
        out_specs=VMEM,
        compiler_params=SMALL,
        name="assemble",
    )(own, keys, values)


def prepare_kernel(
    id_ref,
    len_ref,
    q_hbm,
    g_hbm,
    table_hbm,
    rk_hbm,
    rv_hbm,
    biased_ref,
    masked_ref,
    rk_ref,
    rv_ref,
    table_ref,
    sems,
):
    arrays = [
        (table_hbm, table_ref),
        (q_hbm, biased_ref),
        (g_hbm, masked_ref),
        (rk_hbm, rk_ref),
        (rv_hbm, rv_ref),
    ]
    copies = [pltpu.make_async_copy(a, b, sems.at[i]) for i, (a, b) in enumerate(arrays)]
    for copy in copies:
        copy.start()
    copies[0].wait()
    chosen = lax.broadcasted_iota(jnp.int32, table_ref.shape, 0) == id_ref[0]
    pref = jnp.sum(jnp.where(chosen, table_ref[...].astype(F32), 0.0), axis=0, keepdims=True)
    copies[1].wait()
    biased_ref[...] = (biased_ref[...].astype(F32) + pref).astype(BF16)
    copies[2].wait()
    live = lax.broadcasted_iota(jnp.int32, masked_ref.shape, 0) < len_ref[0]
    masked_ref[...] = jnp.where(live, masked_ref[...], jnp.zeros((), BF16))
    copies[3].wait()
    copies[4].wait()


def prepare(pref_ids, resp_len, queries, out_grad, table, resp_keys, resp_values):
    wide = jax.ShapeDtypeStruct(queries.shape, BF16)
    slim = jax.ShapeDtypeStruct(resp_keys.shape, BF16)
    return pl.pallas_call(
        prepare_kernel,
        out_shape=[wide, wide, slim, slim],
        in_specs=[SMEM, SMEM] + [ANY] * 5,
        out_specs=[VMEM] * 4,
        scratch_shapes=[pltpu.VMEM(table.shape, BF16), pltpu.SemaphoreType.DMA((5,))],
        compiler_params=SMALL,
        cost_estimate=pl.CostEstimate(
            flops=4 * queries.size, bytes_accessed=8 * queries.size, transcendentals=0
        ),
        name="prepare",
    )(pref_ids, resp_len, queries, out_grad, table, resp_keys, resp_values)


def chip_tile(r_ref, mate_ref):
    own = r_ref[...].astype(F32)[: RTILE // 2]
    mate = mate_ref[mate_ref.shape[0] - RTILE :, :].astype(F32)[: RTILE // 2]
    return jnp.concatenate([own, mate], axis=0).astype(BF16)


def pair_sum_kernel(tiles, direct_ref, got_ref, r_ref, mate_ref, *out_refs):
    at = 0
    for out, count in zip(out_refs, tiles):
        n = out.shape[0] - (RTILE if count else 0)
        total = direct_ref[at : at + n, :].astype(F32) + got_ref[at : at + n, :].astype(F32)
        out[:n, :] = total.astype(out.dtype)
        if count == 1:
            out[n:, :] = r_ref[...]
        if count == 2:
            out[n:, :] = chip_tile(r_ref, mate_ref)
        at += n


def pair_sum(direct, got, r_tile, mate, sizes, tiles):
    lanes = direct.shape[1]
    return pl.pallas_call(
        functools.partial(pair_sum_kernel, tiles),
        out_shape=[
            jax.ShapeDtypeStruct((n + RTILE if t else n, lanes), BF16 if t else F32)
            for n, t in zip(sizes, tiles)
        ],
        in_specs=[VMEM] * 4,
        out_specs=[VMEM] * len(sizes),
        compiler_params=SMALL,
        name="pair_sum",
    )(direct, got, r_tile, mate)


def middle_sum_kernel(two_ref, three_ref, four_ref, r_ref, got_ref, out_ref):
    rows = two_ref.shape[0]
    block = rows // 2
    total = two_ref[...] + three_ref[:rows, :].astype(F32)
    out_ref[:block, :] = (total[:block, :] + four_ref[:block, :].astype(F32)).astype(BF16)
    out_ref[block:rows, :] = total[block:, :].astype(BF16)
    out_ref[rows : rows + RTILE, :] = chip_tile(r_ref, got_ref)
    out_ref[rows + RTILE : rows + 2 * RTILE, :] = three_ref[rows:, :]
    out_ref[rows + 2 * RTILE :, :] = four_ref[block:, :]


def middle_sum(two, three, four, r_tile, got):
    return pl.pallas_call(
        middle_sum_kernel,
        out_shape=jax.ShapeDtypeStruct((two.shape[0] + 3 * RTILE, two.shape[1]), BF16),
        in_specs=[VMEM] * 5,
        out_specs=VMEM,
        compiler_params=SMALL,
        name="middle_sum",
    )(two, three, four, r_tile, got)


def chip_sum_kernel(near_ref, one_ref, two_ref, mine_ref, other_ref):
    rows = near_ref.shape[0]
    block = rows // 2
    total = near_ref[...].astype(F32) + one_ref[:rows, :].astype(F32) + two_ref[:rows, :].astype(F32)
    mine_ref[...] = total[:block, :]
    other_ref[:block, :] = total[block:, :].astype(BF16)
    split = block + one_ref.shape[0] - rows
    other_ref[block:split, :] = one_ref[rows:, :]
    other_ref[split:, :] = two_ref[rows:, :]


def chip_sum(near, one, two):
    rows, lanes = near.shape
    block = rows // 2
    sent = block + one.shape[0] + two.shape[0] - 2 * rows
    return pl.pallas_call(
        chip_sum_kernel,
        out_shape=[
            jax.ShapeDtypeStruct((block, lanes), F32),
            jax.ShapeDtypeStruct((sent, lanes), BF16),
        ],
        in_specs=[VMEM] * 3,
        out_specs=[VMEM] * 2,
        compiler_params=SMALL,
        name="chip_sum",
    )(near, one, two)


def flush_kernel(*refs):
    count = len(refs) // 2
    sems = refs[-1]
    copies = [
        pltpu.make_async_copy(refs[i], refs[count + i], sems.at[i]) for i in range(count)
    ]
    for copy in copies:
        copy.start()
    for copy in copies:
        copy.wait()


def flush(arrays):
    return pl.pallas_call(
        flush_kernel,
        out_shape=[jax.ShapeDtypeStruct(a.shape, a.dtype) for a in arrays],
        in_specs=[VMEM] * len(arrays),
        out_specs=[ANY] * len(arrays),
        scratch_shapes=[pltpu.SemaphoreType.DMA((len(arrays),))],
        compiler_params=SMALL,
        name="flush",
    )(*arrays)


def last_sum_kernel(mine_ref, sent_ref, last_ref, r_ref, got_ref, dk_ref, dv_ref, pref_ref):
    block = mine_ref.shape[0]
    total = mine_ref[...] + last_ref[:block, :].astype(F32)
    dk_ref[...] = total[:, :HEAD_DIM].astype(BF16)
    dv_ref[...] = total[:, HEAD_DIM:].astype(BF16)
    n_pref, columns = pref_ref.shape
    lanes = mine_ref.shape[1]
    tiles = [chip_tile(r_ref, got_ref)]
    for ref in (sent_ref, last_ref):
        for at in range(block, ref.shape[0], RTILE):
            tiles.append(ref[at : at + RTILE, :])
    tiles = [t.astype(F32) for t in tiles]
    count = columns // lanes
    half = RTILE // 2
    tiles = [t[at : at + half, :] for t in tiles for at in (0, half)]
    hot = jnp.concatenate([t[count : count + 1, :n_pref] for t in tiles], axis=0)
    hot = hot.astype(BF16)
    for j in range(count):
        sums = jnp.concatenate([t[j : j + 1, :] for t in tiles], axis=0).astype(BF16)
        pref_ref[:, j * lanes : (j + 1) * lanes] = lax.dot_general(
            hot, sums, (((0,), (0,)), ((), ())), preferred_element_type=F32
        )


def last_sum(mine, sent, last, r_tile, got, n_pref, columns):
    block = mine.shape[0]
    return pl.pallas_call(
        last_sum_kernel,
        out_shape=[
            jax.ShapeDtypeStruct((block, HEAD_DIM), BF16),
            jax.ShapeDtypeStruct((block, HEAD_DIM), BF16),
            jax.ShapeDtypeStruct((n_pref, columns), F32),
        ],
        in_specs=[VMEM] * 5,
        out_specs=[VMEM] * 3,
        compiler_params=SMALL,
        name="last_sum",
    )(mine, sent, last, r_tile, got)


def in_hbm(array):
    return pltpu.with_memory_space_constraint(array, pltpu.HBM)


def shards(
    n_resp,
    queries,
    resp_keys,
    resp_values,
    prompt_keys,
    prompt_values,
    out_grad,
    pref_table,
    pref_ids,
    resp_len,
):
    pair, to_one, to_two, to_three, to_four = ring_moves(n_resp)

    def move(array, moves):
        return lax.ppermute(array, "resp", moves)

    block = prompt_keys.shape[0]
    arrays = (queries, out_grad, pref_table, resp_keys, resp_values)
    biased, masked, resp_keys, resp_values = prepare(
        pref_ids, resp_len, *[in_hbm(array) for array in arrays]
    )
    mate = [move(prompt_keys, pair), move(prompt_values, pair)]
    chip = assemble(pack(in_hbm(prompt_keys), in_hbm(prompt_values)), *mate)
    second = move(chip, to_two)
    first = move(chip, to_one)
    part0 = scores(biased, masked, [chip], (resp_keys, resp_values))
    second, part0 = lax.optimization_barrier((second, part0))
    third = move(second, to_three)
    fourth = move(second[:block], to_four)
    part1 = scores(biased, masked, [first, second])
    part2 = scores(biased, masked, [move(first, pair), move(second, pair)])
    third, fourth, part1, part2 = lax.optimization_barrier((third, fourth, part1, part2))
    part3 = scores(biased, masked, [third, fourth])
    part4 = scores(biased, masked, [move(third, pair), move(fourth, pair)])
    parts = [part0, part1, part2, part3, part4]
    lows, dps, stats, keys_t = zip(*parts)
    *ds, query_grad, scale, r_tile = query_side(
        pref_ids, lows, dps, stats, keys_t, queries.shape[0], queries.shape[1]
    )

    def keys_of(picks, near, *extra):
        some_ds, some_lows = [ds[i] for i in picks], [lows[i] for i in picks]
        return key_side(picks, scale, biased, masked, some_ds, some_lows, near, extra)

    direct_far, via_far = keys_of((3, 4), False, r_tile)
    got = move(via_far, pair)
    three, four = pair_sum(direct_far, got, r_tile, got, (2 * block, block), (2, 1))
    (via_close,) = keys_of((2,), False)
    (direct_close,) = keys_of((1,), False)
    one, two = pair_sum(
        direct_close, move(via_close, pair), r_tile, got, (2 * block, 2 * block), (2, 0)
    )
    four = move(four, to_four)
    three = move(three, to_three)
    one = move(one, to_one)
    two = move(middle_sum(two, three, four, r_tile, got), to_two)
    scale, one = lax.optimization_barrier((scale, one))
    near, resp_key_grad, resp_value_grad = keys_of((0,), True)
    mine, sent = chip_sum(near, one, two)
    results = (query_grad, resp_key_grad, resp_value_grad)
    sent, results = lax.optimization_barrier((sent, results))
    query_grad, resp_key_grad, resp_value_grad = flush(results)
    last = move(sent, pair)
    prompt_key_grad, prompt_value_grad, pref_grad = last_sum(
        mine, sent, last, r_tile, got, pref_table.shape[0], queries.shape[1]
    )
    return (
        query_grad,
        resp_key_grad,
        resp_value_grad,
        prompt_key_grad,
        prompt_value_grad,
        pref_grad,
    )


def solution(mesh):
    rows = P(("dp", "resp"), "tensor")
    in_specs = (rows,) * 6 + (P(None, "tensor"), P(("dp", "resp")), P(("dp", "resp")))
    out_specs = (rows,) * 5 + (P("dp", "tensor"),)
    return jax.shard_map(
        functools.partial(shards, mesh.shape["resp"]),
        mesh=mesh,
        in_specs=in_specs,
        out_specs=out_specs,
        check_vma=False,
    )
```
